128 devices in a mesh: dp: 4 (over y), fsdp: 32 (over z, x, core).
Axes of the slice: x: 4, y: 4, z: 4, core: 2. Of those that a mesh axis runs over, the one named last changes fastest.
Arguments:
- grad_parts: bfloat16 [4, 36, 1024, 1024], P('dp', None, 'fsdp'), as said below
- left_stats: float32 [96, 32, 4, 8, 1024], P('fsdp', None, 'dp'), as said below
- right_stats: float32 [96, 32, 4, 8, 1024], P('fsdp', None, 'dp'), as said below
- accum: float32 [96, 32, 4, 8, 1024], P('fsdp', None, 'dp'), may hold values from 0.001 to 0.1
- left_root: bfloat16 [96, 32, 4, 8, 1024], P('fsdp', None, 'dp'), as said below
- right_root: bfloat16 [96, 32, 4, 8, 1024], P('fsdp', None, 'dp'), as said below
- owner_slot: int32 [36], replicated, may hold values from 0 to 95, as said below
Outputs:
- update: bfloat16 [36, 1024, 1024], P(None, 'fsdp')
- left_new: float32 [96, 32, 4, 8, 1024], P('fsdp', None, 'dp')
- right_new: float32 [96, 32, 4, 8, 1024], P('fsdp', None, 'dp')
- accum_new: float32 [96, 32, 4, 8, 1024], P('fsdp', None, 'dp')
The draws below stay inside these ranges and needn't reach their ends.
Inputs may be any that keep to these rules, and one draw needn't show every extreme that they name: Entries are distinct; block b lives on owner owner_slot[b] // 3 in its slot owner_slot[b] % 3; in every draw some owner has all 3 slots in use, which one drawn from the seed. `grad_parts`: each block's rows and columns carry their own scales. `left_stats`: positive diagonal with independent off-diagonal entries. `right_stats`: positive diagonal with independent off-diagonal entries. `left_root`: positive diagonal with independent off-diagonal entries. `right_root`: positive diagonal with independent off-diagonal entries.
All inputs are finite; a program needn't handle non-finite values.
Results may differ from the reference program's by a relative error of at most 0.023.
Values may be sent and summed in bfloat16 or wider, within the bound.
A program may use at most 192 MiB of HBM per device.

```python
import math
import jax
import jax.numpy as jnp
from jax import lax

B = 1024
SLOTS = 3
BLOCKS = 36
OWNERS = 32
OWNED = 96
REPLICAS = 4
SUB = 8


def dominant(key, diag_lo, diag_hi, spread):
    first, second = jax.random.split(key)
    rows = jnp.arange(B).reshape(1, B, 1)
    cols = jnp.arange(B).reshape(1, 1, B)
    diag = jnp.exp(jax.random.uniform(first, (OWNED, B, 1), jnp.float32, math.log(diag_lo), math.log(diag_hi)))
    other = jax.random.normal(second, (OWNED, B, B), jnp.float32) * (spread / math.sqrt(B))
    square = jnp.where(rows == cols, diag, other)
    return square.reshape(OWNED, OWNERS, REPLICAS, SUB, B)


def draw_left_stats(key, part):
    key = jax.random.fold_in(key, 21)
    return dominant(key, 0.5, 5.0, 0.6)


def draw_right_stats(key, part):
    key = jax.random.fold_in(key, 22)
    return dominant(key, 0.5, 5.0, 0.6)


def draw_left_root(key, part):
    key = jax.random.fold_in(key, 23)
    return dominant(key, 0.3, 3.0, 0.4).astype(jnp.bfloat16)


def draw_right_root(key, part):
    key = jax.random.fold_in(key, 24)
    return dominant(key, 0.3, 3.0, 0.4).astype(jnp.bfloat16)


def draw_grad_parts(key, part):
    key = jax.random.fold_in(key, 11)
    first = jax.random.fold_in(key, 0)
    second = jax.random.fold_in(key, 1)
    fourth = jax.random.fold_in(key, 3)
    top = math.log(10.0)
    noise = jnp.clip(jax.random.normal(fourth, (REPLICAS, BLOCKS, B, B), jnp.float32), -4.0, 4.0)
    rows = jnp.exp(jax.random.uniform(first, (1, BLOCKS, B, 1), jnp.float32, 0.0, top))
    cols = jnp.exp(jax.random.uniform(second, (1, BLOCKS, 1, B), jnp.float32, 0.0, top))
    return (0.003 * noise * rows * cols).astype(jnp.bfloat16)


def draw_owner_slot(key, part):
    key = jax.random.fold_in(key, 5)
    first, second, third = jax.random.split(key, 3)
    full_owner = jax.random.randint(first, (), 0, OWNERS)
    order = jax.random.permutation(second, OWNED)
    edge = jnp.logical_or(order == 0, order == OWNED - 1).astype(jnp.int32)
    inside = (order // SLOTS == full_owner).astype(jnp.int32)
    priority = jnp.where(inside == 1, 2, 1 - edge)
    rest = order[jnp.argsort(priority, stable=True)]
    chosen = jnp.concatenate([full_owner * SLOTS + jnp.arange(SLOTS, dtype=jnp.int32), rest[:BLOCKS - SLOTS].astype(jnp.int32)])
    return jax.random.permutation(third, chosen).astype(jnp.int32)


def level_of(own_key, shape, pieces, smallest, top_value):
    def one(axis_at, parts):
        draws = jax.random.uniform(jax.random.fold_in(jax.random.fold_in(own_key, 6), axis_at), (parts,), jnp.float32, smallest / len(pieces), top_value / len(pieces))
        return jnp.repeat(jnp.exp(draws), shape[axis_at] // parts).reshape((-1,) + (1,) * (len(shape) - axis_at - 1))

    level = one(*pieces[0])
    for cut in pieces[1:]:
        level = level * one(*cut)
    return level


def setup_inputs(seed: int = 0) -> dict:
    key_list = jax.random.split(jax.random.key(seed), 8)
    return {
        "grad_parts": draw_grad_parts(jax.random.fold_in(key_list[7], 71), 0),
        "left_stats": draw_left_stats(jax.random.fold_in(key_list[7], 71), 0),
        "right_stats": draw_right_stats(jax.random.fold_in(key_list[7], 71), 0),
        "accum": jnp.clip(jnp.exp(math.log(0.1) - 4.6051702 * jax.random.uniform(key_list[3], (OWNED, OWNERS, REPLICAS, SUB, B), jnp.float32) ** level_of(key_list[3], (OWNED, OWNERS, REPLICAS, SUB, B), ((0, 32), (2, 4)), -0.2, 0.2)), 0.001, 0.1),
        "left_root": draw_left_root(jax.random.fold_in(key_list[7], 71), 0),
        "right_root": draw_right_root(jax.random.fold_in(key_list[7], 71), 0),
        "owner_slot": draw_owner_slot(jax.random.fold_in(key_list[7], 71), 0),
    }


def reference(grad_parts, left_stats, right_stats, accum, left_root, right_root, owner_slot):
    grads = lax.optimization_barrier(jnp.sum(grad_parts.astype(jnp.float32), axis=0)).astype(jnp.bfloat16)
    slot_grads = jnp.zeros((OWNED, B, B), jnp.bfloat16).at[owner_slot].set(grads)

    def square(array):
        return array.reshape(OWNED, B, B)

    def one_slot(items):
        grad, left, right, accu, lroot, rroot = items
        left_out = 0.95 * left + 0.05 * jnp.dot(grad, grad.T, preferred_element_type=jnp.float32)
        right_out = 0.95 * right + 0.05 * jnp.dot(grad.T, grad, preferred_element_type=jnp.float32)
        wide = grad.astype(jnp.float32)
        accu_out = accu + wide * wide
        direction = wide / jnp.sqrt(accu_out)
        half = jnp.dot(lroot, grad, preferred_element_type=jnp.float32).astype(jnp.bfloat16)
        precond = jnp.dot(half, rroot, preferred_element_type=jnp.float32)
        dnorm = jnp.sum(direction * direction)
        pnorm = jnp.sum(precond * precond)
        slot_update = (precond * jnp.sqrt(dnorm / (pnorm + 1e-06))).astype(jnp.bfloat16)
        return (slot_update, left_out, right_out, accu_out)
    slot_update, left_out, right_out, accu_out = lax.map(one_slot, (slot_grads, square(left_stats), square(right_stats), square(accum), square(left_root), square(right_root)))
    update = slot_update[owner_slot]
    layout = (OWNED, OWNERS, REPLICAS, SUB, B)
    return (update, left_out.reshape(layout), right_out.reshape(layout), accu_out.reshape(layout))
```

```python
import functools

import jax
import jax.numpy as jnp
from jax import lax
from jax.experimental import pallas as pl
from jax.experimental.pallas import tpu as pltpu
from jax.sharding import PartitionSpec as P

MESH = pl.DeviceIdType.MESH
BF = jnp.bfloat16
F32 = jnp.float32
STEP = 13


def dot(a, b):
    return jnp.dot(a, b, preferred_element_type=F32)


def dot_t(a, b):
    return lax.dot_general(a, b, (((1,), (1,)), ((), ())), preferred_element_type=F32)


def step_kernel(
    N, S, F, W,
    inv_ref, pick_ref, gp, lr, rr, ac,
    sl_out, sr_out, gm_out, up_out,
    ra, rb, fa_raw, fb_raw, ca, cb, fa_comb, fb_comb,
    red_own, red_l, red_r, red_o,
    sb, gb, rraw, rn, lv, av, sel, hf, pv, gct, gmb, ls, rs_,
    pb, u, uall, nb,
    rs_s, rs_r, ag_s, ag_r, rt_s, rt_r, g_s, g_r, p_s, p_r, n_s, n_r, u_s, u_r, loc, outs,
):
    H = N // 2
    W2 = W // 2
    B = F * 32
    SH = F * 8
    T = 256 if W % 256 == 0 else W
    NT = W // T
    nx = 4 if F >= 32 else 2
    nz = F // (2 * nx)
    d = lax.axis_index("dp")
    f = lax.axis_index("fsdp")
    z = f // (2 * nx)
    x = (f // 2) % nx
    c = f % 2
    e1, e2, e3 = lax.rem(d + 1, 4), lax.rem(d + 2, 4), lax.rem(d + 3, 4)
    right, left, opp = (e1, f), (e3, f), (e2, f)
    lo, hi = pl.ds(0, H), pl.ds(H, H)

    def peer(i):
        o = lax.rem(i * STEP, F)
        pz = lax.rem(z + o // (2 * nx), nz)
        px = lax.rem(x + (o // 2) % nx, nx)
        pc = lax.rem(c + o % 2, 2)
        return (pz * nx + px) * 2 + pc

    def rcopy(src, dst, ss, rs, dev):
        return pltpu.make_async_remote_copy(
            src_ref=src, dst_ref=dst, send_sem=ss, recv_sem=rs, device_id=dev, device_id_type=MESH
        )

    def rows(e):
        return pl.ds(pl.multiple_of((e // 2) * 16, 16), 16)

    def cols(e):
        return pl.ds(pl.multiple_of((e % 2) * W2, W2), W2)

    def loop(n, fn, unroll=1):
        lax.fori_loop(0, n, lambda i, _: (fn(i), 0)[1], 0, unroll=unroll)

    ld_l = pltpu.make_async_copy(lr, lv, loc.at[0])
    ld_l.start()
    ld_a = pltpu.make_async_copy(ac, av, loc.at[1])
    ld_a.start()
    ld_r = pltpu.make_async_copy(rr, rraw.at[d], loc.at[2])
    ld_r.start()

    barrier = pltpu.get_barrier_semaphore()

    def greet(i):
        pl.semaphore_signal(barrier, inc=1, device_id=(d, peer(i + 1)), device_id_type=MESH)

    for dev in (right, left, opp):
        pl.semaphore_signal(barrier, inc=1, device_id=dev, device_id_type=MESH)
    loop(F - 1, greet)
    for ref in (red_own, red_l, red_r, red_o):
        ref[N] = jnp.zeros((16, W2), BF)
    pick = lax.broadcasted_iota(jnp.int32, (SH, B), 0)
    at = lax.broadcasted_iota(jnp.int32, (SH, B), 1)
    sel[...] = jnp.where(at == (pick // 8) * 32 + d * 8 + pick % 8, 1.0, 0.0).astype(BF)
    pl.semaphore_wait(barrier, F + 2)

    c1 = rcopy(gp.at[lo, rows(e2), cols(e2)], ra, rs_s.at[0], rs_r.at[0], right)
    c2 = rcopy(gp.at[hi, rows(e2), cols(e2)], rb, rs_s.at[1], rs_r.at[1], left)
    c3 = rcopy(gp.at[hi, rows(e1), cols(e1)], fb_raw, rs_s.at[2], rs_r.at[2], right)
    c4 = rcopy(gp.at[lo, rows(e3), cols(e3)], fa_raw, rs_s.at[3], rs_r.at[3], left)
    c5 = rcopy(ca, fa_comb, rs_s.at[4], rs_r.at[4], right)
    c6 = rcopy(cb, fb_comb, rs_s.at[5], rs_r.at[5], left)
    c1.start()
    c2.start()
    c3.start()
    c4.start()
    c1.wait_recv()

    def add_a(b):
        ca[b] = (ra[b].astype(F32) + gp[b, rows(e1), cols(e1)].astype(F32)).astype(BF)

    loop(H, add_a)
    c5.start()
    c2.wait_recv()

    def add_b(b):
        cb[b] = (rb[b].astype(F32) + gp[H + b, rows(e3), cols(e3)].astype(F32)).astype(BF)

    loop(H, add_b)
    c6.start()
    c4.wait_recv()
    c5.wait_recv()

    def fin_a(b):
        own = gp[b, rows(d), cols(d)].astype(F32)
        red_own[b] = (own + fa_raw[b].astype(F32) + fa_comb[b].astype(F32)).astype(BF)

    loop(H, fin_a)
    c3.wait_recv()
    c6.wait_recv()

    def fin_b(b):
        own = gp[H + b, rows(d), cols(d)].astype(F32)
        red_own[H + b] = (own + fb_raw[b].astype(F32) + fb_comb[b].astype(F32)).astype(BF)

    loop(H, fin_b)

    every = pl.ds(0, N)
    a1 = rcopy(red_own.at[every], red_l.at[every], ag_s.at[0], ag_r.at[0], right)
    a2 = rcopy(red_own.at[every], red_r.at[every], ag_s.at[1], ag_r.at[1], left)
    a3 = rcopy(red_l.at[lo], red_o.at[lo], ag_s.at[2], ag_r.at[2], right)
    a4 = rcopy(red_r.at[hi], red_o.at[hi], ag_s.at[3], ag_r.at[3], left)
    a1.start()
    a2.start()

    HR = SH // 2
    up_, dn_ = pl.ds(0, HR), pl.ds(HR, HR)

    def root(s):
        return (
            rcopy(rr.at[s], rraw.at[d, s], rt_s.at[s, 0], rt_r.at[s, 0], right),
            rcopy(rr.at[s], rraw.at[d, s], rt_s.at[s, 1], rt_r.at[s, 1], left),
            rcopy(rraw.at[e3, s, up_], rraw.at[e3, s, up_], rt_s.at[s, 2], rt_r.at[s, 2], right),
            rcopy(rraw.at[e1, s, dn_], rraw.at[e1, s, dn_], rt_s.at[s, 3], rt_r.at[s, 3], left),
        )

    roots = [root(s) for s in range(S)]

    def start_root(s):
        roots[s][0].start()
        roots[s][1].start()

    def forward_root(s):
        roots[s][0].wait_recv()
        roots[s][2].start()
        roots[s][1].wait_recv()
        roots[s][3].start()

    def place(red, e):
        def one(q):
            for s in range(S):
                sb[s, q, rows(e), cols(e)] = red[inv_ref[q * S + s]]

        loop(F, one)

    def send_quarter(s, e):
        def one(i):
            q = peer(i + 1)
            rcopy(
                sb.at[s, q, rows(e), cols(e)],
                gb.at[s, f, rows(e), cols(e)],
                g_s.at[s], g_r.at[s], (d, q),
            ).start()

        loop(F - 1, one)

    def send_whole(s):
        def one(i):
            q = peer(i + 1)
            rcopy(sb.at[s, q], gb.at[s, f], g_s.at[s], g_r.at[s], (d, q)).start()

        loop(F - 1, one)

    place(red_own, d)
    send_quarter(0, d)
    a1.wait_recv()
    a3.start()
    a2.wait_recv()
    a4.start()
    start_root(0)
    place(red_l, e3)
    send_quarter(0, e3)
    place(red_r, e1)
    send_quarter(0, e1)
    a3.wait_recv()
    a4.wait_recv()
    place(red_o, e2)
    send_quarter(0, e2)
    selfs = [pltpu.make_async_copy(sb.at[s, f], gb.at[s, f], loc.at[3 + s]) for s in range(S)]
    for s in range(S):
        selfs[s].start()
    for s in range(1, S):
        send_whole(s)
    forward_root(0)
    if S > 1:
        start_root(1)
    ld_l.wait()
    ld_a.wait()
    ld_r.wait()

    def tile(j):
        return pl.ds(pl.multiple_of(j * T, T), T)

    def gcols(s, j):
        return gb[s, :, :, tile(j)].reshape(B, T)

    def grows(s, j):
        return gb[s, pl.ds(j * (T // 32), T // 32)].reshape(T, W)

    out_copies = []

    def put(src, dst, k):
        cp = pltpu.make_async_copy(src, dst, outs.at[k])
        cp.start()
        out_copies.append(cp)

    def others(n):
        return pl.ds(0, n)

    for s in range(S):
        rcopy(sb.at[s, others(F - 1)], gb.at[s, others(F - 1)], g_s.at[s], g_r.at[s], right).wait_recv()
        selfs[s].wait()

        def mine(j, dn):
            g = dot(sel[...], gcols(s, j))
            gmb[s, :, tile(j)] = g.astype(BF)
            an = av[s, :, tile(j)] + g * g
            dr = g * lax.rsqrt(an)
            return dn + jnp.sum(dr * dr)

        dn = lax.fori_loop(0, NT, mine, jnp.float32(0))

        def halves(j):
            hf[:, tile(j)] = dot(lv[s], gcols(s, j)).astype(BF)

        loop(NT, halves)

        roots[s][2].wait_recv()
        roots[s][3].wait_recv()

        def weave(t):
            part = [rraw[e, s, pl.ds(pl.multiple_of(t * 16, 16), 16), :].astype(F32) for e in range(4)]
            for h in range(2):
                rows32 = jnp.concatenate([p[8 * h : 8 * h + 8] for p in part], axis=0)
                rn[pl.ds(pl.multiple_of(t * 64 + 32 * h, 32), 32), :] = rows32.astype(BF)

        loop(F // 2, weave)

        def prec(j, pn):
            p = dot(hf[...], rn[:, tile(j)])
            pv[:, tile(j)] = p
            return pn + jnp.sum(p * p)

        pn = lax.fori_loop(0, NT, prec, jnp.float32(0))

        nb[s, d, 0] = jnp.full((8, 128), dn, F32)
        nb[s, d, 1] = jnp.full((8, 128), pn, F32)
        ns = [
            rcopy(nb.at[s, d], nb.at[s, d], n_s.at[s, k], n_r.at[s, k], dev)
            for k, dev in enumerate((right, left, opp))
        ]
        for cp in ns:
            cp.start()
        if s + 1 < S:
            forward_root(s + 1)
            if s + 2 < S:
                start_root(s + 2)
        for cp in ns:
            cp.wait()
        dsum = nb[s, 0, 0] + nb[s, 1, 0] + nb[s, 2, 0] + nb[s, 3, 0]
        psum = nb[s, 0, 1] + nb[s, 1, 1] + nb[s, 2, 1] + nb[s, 3, 1]
        factor = jnp.sqrt(dsum / (psum + 1e-06))[0:1, 0:1]

        def scale(q):
            v = pv[pl.ds(pl.multiple_of(q * 8, 8), 8), :] * factor
            pb[s, q] = jnp.concatenate([v[:, :W2], v[:, W2:]], axis=0).astype(BF)

        loop(F, scale)
        u[s * F + f] = pb[s, f]

        def send_p(i):
            q = peer(i + 1)
            rcopy(pb.at[s, q], u.at[s * F + f], p_s.at[s], p_r.at[s], (d, q)).start()

        loop(F - 1, send_p)

        def left_stat(j):
            g = grows(s, j)
            ls[s, :, tile(j)] = dot_t(gmb[s], g).astype(BF)
            gct[:, tile(j)] = dot_t(sel[...], g).astype(BF)

        loop(NT, left_stat)

        def right_stat(j):
            rs_[s, :, tile(j)] = dot(gct[...], gcols(s, j)).astype(BF)

        loop(NT, right_stat)
        put(gmb.at[s], gm_out.at[s], 3 * s)
        put(ls.at[s], sl_out.at[s], 3 * s + 1)
        put(rs_.at[s], sr_out.at[s], 3 * s + 2)

    for s in range(S):
        rcopy(
            pb.at[s, others(F - 1)], u.at[pl.ds(s * F, F - 1)], p_s.at[s], p_r.at[s], right
        ).wait_recv()

    def choose(b):
        uall[d, b] = u[pick_ref[b]]

    loop(N, choose)
    u1 = rcopy(uall.at[d], uall.at[d], u_s.at[0], u_r.at[0], right)
    u2 = rcopy(uall.at[d], uall.at[d], u_s.at[1], u_r.at[1], left)
    u3 = rcopy(uall.at[e3, lo], uall.at[e3, lo], u_s.at[2], u_r.at[2], right)
    u4 = rcopy(uall.at[e1, hi], uall.at[e1, hi], u_s.at[3], u_r.at[3], left)
    u1.start()
    u2.start()
    put(uall.at[d], up_out.at[d], 3 * S)
    u1.wait_recv()
    u3.start()
    put(uall.at[e3], up_out.at[e3], 3 * S + 1)
    u2.wait_recv()
    u4.start()
    put(uall.at[e1], up_out.at[e1], 3 * S + 2)
    u3.wait_recv()
    u4.wait_recv()
    put(uall.at[e2], up_out.at[e2], 3 * S + 3)

    for cp in (c1, c2, c3, c4, c5, c6, a1, a2, a3, a4, u1, u2, u3, u4):
        cp.wait_send()
    for s in range(S):
        for cp in roots[s]:
            cp.wait_send()
        rcopy(sb.at[s, others(F - 1)], gb.at[s, others(F - 1)], g_s.at[s], g_r.at[s], right).wait_send()
        rcopy(pb.at[s, others(F - 1)], u.at[pl.ds(s * F, F - 1)], p_s.at[s], p_r.at[s], right).wait_send()
    for cp in out_copies:
        cp.wait()


def finish_kernel(up, sl, sr, gm, left, right, acc, up_o, left_o, right_o, acc_o):
    n = up.shape[1]
    for b in range(n):
        parts = []
        for e in range(4):
            v = up[e, b].astype(F32)
            parts.append(jnp.concatenate([v[:8], v[8:]], axis=1))
        up_o[b] = jnp.concatenate(parts, axis=0).astype(BF)
    left_o[...] = 0.95 * left[...] + 0.05 * sl[...].astype(F32)
    right_o[...] = 0.95 * right[...] + 0.05 * sr[...].astype(F32)
    g = gm[...].astype(F32)
    acc_o[...] = acc[...] + g * g


def body(grad_parts, left_stats, right_stats, accum, left_root, right_root, owner_slot):
    N = owner_slot.shape[0]
    F = lax.axis_size("fsdp")
    S = left_stats.shape[0]
    W = left_stats.shape[4]
    SH = F * 8
    H = N // 2
    W2 = W // 2
    G = F * S
    slots = lax.broadcasted_iota(jnp.int32, (G, N), 0)
    blocks = lax.broadcasted_iota(jnp.int32, (G, N), 1)
    inv = jnp.min(jnp.where(slots == owner_slot[None, :], blocks, N), axis=1)
    pick = (owner_slot % S) * F + owner_slot // S
    hbm = pl.BlockSpec(memory_space=pl.ANY)
    vmem = pl.BlockSpec(memory_space=pltpu.VMEM)
    smem = pl.BlockSpec(memory_space=pltpu.SMEM)
    half = pltpu.VMEM((H, 16, W2), BF)
    whole = pltpu.VMEM((N + 1, 16, W2), BF)
    dma = pltpu.SemaphoreType.DMA
    share = jax.ShapeDtypeStruct((S, SH, W), BF)
    sl, sr, gm, up = pl.pallas_call(
        functools.partial(step_kernel, N, S, F, W),
        out_shape=(share, share, share, jax.ShapeDtypeStruct((4, N, 16, W2), BF)),
        in_specs=[smem, smem, vmem, hbm, hbm, hbm],
        out_specs=(hbm, hbm, hbm, hbm),
        scratch_shapes=[half] * 8
        + [whole] * 4
        + [
            pltpu.VMEM((S, F, 32, W), BF),
            pltpu.VMEM((S, F, 32, W), BF),
            pltpu.VMEM((4, S, SH, W), BF),
            pltpu.VMEM((F * 32, W), BF),
            pltpu.VMEM((S, SH, W), BF),
            pltpu.VMEM((S, SH, W), F32),
            pltpu.VMEM((SH, F * 32), BF),
            pltpu.VMEM((SH, W), BF),
            pltpu.VMEM((SH, W), F32),
            pltpu.VMEM((SH, F * 32), BF),
            pltpu.VMEM((S, SH, W), BF),
            pltpu.VMEM((S, SH, W), BF),
            pltpu.VMEM((S, SH, W), BF),
            pltpu.VMEM((S, F, 16, W2), BF),
            pltpu.VMEM((S * F, 16, W2), BF),
            pltpu.VMEM((4, N, 16, W2), BF),
            pltpu.VMEM((S, 4, 2, 8, 128), F32),
        ]
        + [
            dma((6,)), dma((6,)), dma((4,)), dma((4,)), dma((S, 4)), dma((S, 4)),
            dma((S,)), dma((S,)), dma((S,)), dma((S,)), dma((S, 3)), dma((S, 3)),
            dma((4,)), dma((4,)), dma((3 + S,)), dma((3 * S + 4,)),
        ],
        compiler_params=pltpu.CompilerParams(
            collective_id=0, has_side_effects=True, vmem_limit_bytes=60 << 20
        ),
        name="shampoo_step",
    )(
        inv, pick, grad_parts[0],
        left_root.reshape(S, SH, W), right_root.reshape(S, SH, W), accum.reshape(S, SH, W),
    )
    rows = S * SH
    K = 12 if N % 12 == 0 and rows % 12 == 0 and (rows // 12) % 16 == 0 else 1
    nb, rb = N // K, rows // K
    flat = pl.BlockSpec((rb, W), lambda i: (i, 0))
    stat = jax.ShapeDtypeStruct((rows, W), F32)
    update, left_out, right_out, accu_out = pl.pallas_call(
        finish_kernel,
        grid=(K,),
        out_shape=(jax.ShapeDtypeStruct((N, 32, W), BF), stat, stat, stat),
        in_specs=[pl.BlockSpec((4, nb, 16, W2), lambda i: (0, i, 0, 0))] + [flat] * 6,
        out_specs=(pl.BlockSpec((nb, 32, W), lambda i: (i, 0, 0)), flat, flat, flat),
        compiler_params=pltpu.CompilerParams(vmem_limit_bytes=32 << 20),
        name="shampoo_finish",
    )(
        up, sl.reshape(rows, W), sr.reshape(rows, W), gm.reshape(rows, W),
        left_stats.reshape(rows, W), right_stats.reshape(rows, W), accum.reshape(rows, W),
    )
    layout = left_stats.shape
    return (update, left_out.reshape(layout), right_out.reshape(layout), accu_out.reshape(layout))


def solution(mesh):
    spread = P("fsdp", None, "dp", None, None)
    return jax.shard_map(
        body,
        mesh=mesh,
        in_specs=(P("dp", None, "fsdp", None),) + (spread,) * 5 + (P(),),
        out_specs=(P(None, "fsdp", None), spread, spread, spread),
        check_vma=False,
    )
```

```python
import functools

import jax
import jax.numpy as jnp
from jax import lax
from jax.experimental import pallas as pl
from jax.experimental.pallas import tpu as pltpu
from jax.sharding import PartitionSpec as P

MESH = pl.DeviceIdType.MESH
BF = jnp.bfloat16
F32 = jnp.float32
STEP = 13
STEP_VMEM = 60 << 20
FINISH_VMEM = 60 << 20


def dot(a, b):
    return jnp.dot(a, b, preferred_element_type=F32)


def dot_t(a, b):
    return lax.dot_general(a, b, (((1,), (1,)), ((), ())), preferred_element_type=F32)


def step_kernel(
    N, S, F, W,
    own_ref, gp, lr, rr, ac,
    sl_out, sr_out, gm_out, up_out, tab_out,
    ra, rb, fa_raw, fb_raw, ca, cb, fa_comb, fb_comb,
    red_own, red_l, red_r, red_o,
    sb, gb, rraw, rn, rv, lv, av, sel, hf, pv, gct, gmb, ls, rs_,
    pb, u_0, u_1, u_2, uall, nb, tab_v, tab,
    rs_s, rs_r, ag_s, ag_r, rt_s, rt_r, g_s, g_r, p_s, p_r, n_s, n_r, u_s, u_r, loc, outs,
):
    H = N // 2
    W2 = W // 2
    B = F * 32
    SH = F * 8
    T = 256 if W % 256 == 0 else W
    NT = W // T
    nx = 4 if F >= 32 else 2
    nz = F // (2 * nx)
    d = lax.axis_index("dp")
    f = lax.axis_index("fsdp")
    z = f // (2 * nx)
    x = (f // 2) % nx
    c = f % 2
    e1, e2, e3 = lax.rem(d + 1, 4), lax.rem(d + 2, 4), lax.rem(d + 3, 4)
    right, left, opp = (e1, f), (e3, f), (e2, f)
    lo, hi = pl.ds(0, H), pl.ds(H, H)

    def peer(i):
        o = lax.rem(i * STEP, F)
        pz = lax.rem(z + o // (2 * nx), nz)
        px = lax.rem(x + (o // 2) % nx, nx)
        pc = lax.rem(c + o % 2, 2)
        return (pz * nx + px) * 2 + pc

    def rcopy(src, dst, ss, rs, dev):
        return pltpu.make_async_remote_copy(
            src_ref=src, dst_ref=dst, send_sem=ss, recv_sem=rs, device_id=dev, device_id_type=MESH
        )

    def rows(e):
        return pl.ds(pl.multiple_of((e // 2) * 16, 16), 16)

    def cols(e):
        return pl.ds(pl.multiple_of((e % 2) * W2, W2), W2)

    def within(v, top):
        return jnp.minimum(jnp.maximum(v, 0), top)

    def loop(n, fn, unroll=1):
        lax.fori_loop(0, n, lambda i, _: (fn(i), 0)[1], 0, unroll=unroll)

    ld_l = pltpu.make_async_copy(lr, lv, loc.at[0])
    ld_l.start()
    ld_a = pltpu.make_async_copy(ac, av, loc.at[1])
    ld_a.start()
    ld_r = pltpu.make_async_copy(rr, rv, loc.at[2])
    ld_r.start()

    barrier = pltpu.get_barrier_semaphore()

    def greet(i):
        pl.semaphore_signal(barrier, inc=1, device_id=(d, peer(i + 1)), device_id_type=MESH)

    for dev in (right, left, opp):
        pl.semaphore_signal(barrier, inc=1, device_id=dev, device_id_type=MESH)
    loop(F - 1, greet)
    for ref in (red_own, red_l, red_r, red_o):
        ref[N] = jnp.zeros((16, W2), BF)
    us = (u_0, u_1, u_2)
    for ref in us:
        ref[F] = jnp.zeros((16, W2), BF)
    pick = lax.broadcasted_iota(jnp.int32, (SH, B), 0)
    at = lax.broadcasted_iota(jnp.int32, (SH, B), 1)
    sel[...] = jnp.where(at == (pick // 8) * 32 + d * 8 + pick % 8, 1.0, 0.0).astype(BF)
    pl.semaphore_wait(barrier, F + 2)

    def tables():
        lanes = 128

        def iota(shape, dim):
            return lax.broadcasted_iota(jnp.int32, shape, dim).astype(F32)

        def count(cond, axis):
            return jnp.sum(jnp.where(cond, 1.0, 0.0), axis=axis, keepdims=True)

        down, along = iota((N, N), 0), iota((N, N), 1)
        own_r = own_ref[...].astype(F32)
        own_rr = jnp.broadcast_to(own_r, (N, N))
        own_c = jnp.sum(jnp.where(down == along, own_rr, 0.0), axis=1, keepdims=True)
        own_cc = jnp.broadcast_to(own_c, (N, N))
        q_r = jnp.floor((own_r + 0.5) * (1.0 / S))
        q_c = jnp.floor((own_c + 0.5) * (1.0 / S))
        same = jnp.broadcast_to(q_c, (N, N)) == jnp.broadcast_to(q_r, (N, N))
        rank_r = count(same & (own_cc < own_rr), 0)
        rank_c = count(same & (own_rr < own_cc), 1)
        rk_r = jnp.broadcast_to(rank_r, (N, N))
        rk_c = jnp.broadcast_to(rank_c, (N, N))
        pos_r = count((rk_c < rk_r) | ((rk_c == rk_r) & (down < along)), 0)
        pos_c = count((rk_r < rk_c) | ((rk_r == rk_c) & (along < down)), 1)
        lane = iota((N, lanes), 1)
        block = iota((N, lanes), 0)
        lane_q = jnp.floor((lane + 0.5) * (1.0 / S))
        lane_r = lane - S * lane_q
        qw = jnp.broadcast_to(q_c, (N, lanes))
        rw = jnp.broadcast_to(rank_c, (N, lanes))
        ow = jnp.broadcast_to(own_c, (N, lanes))
        pw = jnp.broadcast_to(pos_c, (N, lanes))
        inv = jnp.min(
            jnp.where((qw == lane_q) & (rw == lane_r), block, float(N)), axis=0, keepdims=True
        )
        ord_q = jnp.sum(jnp.where(pw == lane, qw, 0.0), axis=0, keepdims=True)
        ord_r = jnp.sum(jnp.where(pw == lane, rw, 0.0), axis=0, keepdims=True)
        base = (f * S).astype(F32)
        here = qw == f.astype(F32)
        total = count(here, 0)
        low = count(here & (ow < base + lane), 0)
        used = count(ow == base + lane, 0)
        rank_s = jnp.where(used > 0.5, low, total + lane[0:1] - low)
        tab_v[0:1, :] = inv.astype(jnp.int32)
        tab_v[1:2, :] = ord_q.astype(jnp.int32)
        tab_v[2:3, :] = ord_r.astype(jnp.int32)
        tab_v[3:4, :] = rank_s.astype(jnp.int32)
        tab_v[4:5, :] = jnp.zeros((1, lanes), jnp.int32)
        tab_v[4:5, 0:N] = pos_r.astype(jnp.int32)
        tab_v[5:8, :] = jnp.zeros((3, lanes), jnp.int32)

    c1 = rcopy(gp.at[lo, rows(e2), cols(e2)], ra, rs_s.at[0], rs_r.at[0], right)
    c2 = rcopy(gp.at[hi, rows(e2), cols(e2)], rb, rs_s.at[1], rs_r.at[1], left)
    c3 = rcopy(gp.at[hi, rows(e1), cols(e1)], fb_raw, rs_s.at[2], rs_r.at[2], right)
    c4 = rcopy(gp.at[lo, rows(e3), cols(e3)], fa_raw, rs_s.at[3], rs_r.at[3], left)
    c5 = rcopy(ca, fa_comb, rs_s.at[4], rs_r.at[4], right)
    c6 = rcopy(cb, fb_comb, rs_s.at[5], rs_r.at[5], left)
    c1.start()
    c2.start()
    c3.start()
    c4.start()
    tables()
    to_scalars = pltpu.make_async_copy(tab_v, tab, loc.at[3 + S])
    to_scalars.start()
    to_scalars.wait()
    perm = []
    for r in range(S):
        k = jnp.int32(0)
        for s in range(1, S):
            k = jnp.where(tab[3, s] == r, s, k)
        perm.append(within(k, S - 1))
    ld_r.wait()

    def reorder(t):
        part = pl.ds(pl.multiple_of(t * 16, 16), 16)
        for r in range(S):
            rraw[d, r, part, :] = rv[perm[r], part, :]

    loop(SH // 16, reorder)
    c1.wait_recv()

    def add_a(b):
        ca[b] = (ra[b].astype(F32) + gp[b, rows(e1), cols(e1)].astype(F32)).astype(BF)

    loop(H, add_a)
    c5.start()
    c2.wait_recv()

    def add_b(b):
        cb[b] = (rb[b].astype(F32) + gp[H + b, rows(e3), cols(e3)].astype(F32)).astype(BF)

    loop(H, add_b)
    c6.start()
    c4.wait_recv()
    c5.wait_recv()

    def fin_a(b):
        own = gp[b, rows(d), cols(d)].astype(F32)
        red_own[b] = (own + fa_raw[b].astype(F32) + fa_comb[b].astype(F32)).astype(BF)

    loop(H, fin_a)
    c3.wait_recv()
    c6.wait_recv()

    def fin_b(b):
        own = gp[H + b, rows(d), cols(d)].astype(F32)
        red_own[H + b] = (own + fb_raw[b].astype(F32) + fb_comb[b].astype(F32)).astype(BF)

    loop(H, fin_b)

    every = pl.ds(0, N)
    a1 = rcopy(red_own.at[every], red_l.at[every], ag_s.at[0], ag_r.at[0], right)
    a2 = rcopy(red_own.at[every], red_r.at[every], ag_s.at[1], ag_r.at[1], left)
    a3 = rcopy(red_l.at[lo], red_o.at[lo], ag_s.at[2], ag_r.at[2], right)
    a4 = rcopy(red_r.at[hi], red_o.at[hi], ag_s.at[3], ag_r.at[3], left)
    a1.start()
    a2.start()

    HR = SH // 2
    up_, dn_ = pl.ds(0, HR), pl.ds(HR, HR)

    def root(s):
        return (
            rcopy(rraw.at[d, s], rraw.at[d, s], rt_s.at[s, 0], rt_r.at[s, 0], right),
            rcopy(rraw.at[d, s], rraw.at[d, s], rt_s.at[s, 1], rt_r.at[s, 1], left),
            rcopy(rraw.at[e3, s, up_], rraw.at[e3, s, up_], rt_s.at[s, 2], rt_r.at[s, 2], right),
            rcopy(rraw.at[e1, s, dn_], rraw.at[e1, s, dn_], rt_s.at[s, 3], rt_r.at[s, 3], left),
        )

    roots = [root(s) for s in range(S)]

    def start_root(s):
        roots[s][0].start()
        roots[s][1].start()

    def forward_root(s):
        roots[s][0].wait_recv()
        roots[s][2].start()
        roots[s][1].wait_recv()
        roots[s][3].start()

    def place(red, e):
        def one(q):
            for s in range(S):
                sb[s, q, rows(e), cols(e)] = red[within(tab[0, q * S + s], N)]

        loop(F, one)

    def send_quarter(s, e):
        def one(i):
            q = peer(i + 1)
            rcopy(
                sb.at[s, q, rows(e), cols(e)],
                gb.at[s, f, rows(e), cols(e)],
                g_s.at[s], g_r.at[s], (d, q),
            ).start()

        loop(F - 1, one)

    def send_whole(s):
        def one(i):
            q = peer(i + 1)
            rcopy(sb.at[s, q], gb.at[s, f], g_s.at[s], g_r.at[s], (d, q)).start()

        loop(F - 1, one)

    place(red_own, d)
    send_quarter(0, d)
    a1.wait_recv()
    a3.start()
    a2.wait_recv()
    a4.start()
    start_root(0)
    place(red_l, e3)
    send_quarter(0, e3)
    place(red_r, e1)
    send_quarter(0, e1)
    a3.wait_recv()
    a4.wait_recv()
    place(red_o, e2)
    send_quarter(0, e2)
    selfs = [pltpu.make_async_copy(sb.at[s, f], gb.at[s, f], loc.at[3 + s]) for s in range(S)]
    for s in range(S):
        selfs[s].start()
    for s in range(1, S):
        send_whole(s)
    forward_root(0)
    if S > 1:
        start_root(1)
    ld_l.wait()
    ld_a.wait()

    def tile(j):
        return pl.ds(pl.multiple_of(j * T, T), T)

    def gcols(s, j):
        return gb[s, :, :, tile(j)].reshape(B, T)

    def grows(s, j):
        return gb[s, pl.ds(j * (T // 32), T // 32)].reshape(T, W)

    out_copies = []

    def put(src, dst, k):
        cp = pltpu.make_async_copy(src, dst, outs.at[k])
        cp.start()
        out_copies.append(cp)

    def others(n):
        return pl.ds(0, n)

    def third(t):
        n = N // S
        own = pl.ds(t * n, n)
        a, b = pl.ds(t * n, n // 2), pl.ds(t * n + n // 2, n - n // 2)
        return (
            rcopy(uall.at[d, own], uall.at[d, own], u_s.at[t, 0], u_r.at[t, 0], right),
            rcopy(uall.at[d, own], uall.at[d, own], u_s.at[t, 1], u_r.at[t, 1], left),
            rcopy(uall.at[e3, a], uall.at[e3, a], u_s.at[t, 2], u_r.at[t, 2], right),
            rcopy(uall.at[e1, b], uall.at[e1, b], u_s.at[t, 3], u_r.at[t, 3], left),
        )

    up_copies = [third(t) for t in range(S)]

    def start_third(t):
        rcopy(
            pb.at[t, others(F - 1)], us[t].at[others(F - 1)], p_s.at[t], p_r.at[t], right
        ).wait_recv()

        def choose(i):
            j = t * (N // S) + i
            q, r = within(tab[1, j], F), tab[2, j]
            v = us[0][jnp.where(r == 0, q, F)].astype(F32)
            for k in range(1, t + 1):
                v = v + us[k][jnp.where(r == k, q, F)].astype(F32)
            uall[d, j] = v.astype(BF)

        loop(N // S, choose)
        up_copies[t][0].start()
        up_copies[t][1].start()

    def forward_third(t):
        up_copies[t][0].wait_recv()
        up_copies[t][2].start()
        up_copies[t][1].wait_recv()
        up_copies[t][3].start()

    def statistics(s):
        def left_stat(j):
            g = grows(s, j)
            ls[s, :, tile(j)] = dot_t(gmb[s], g).astype(BF)
            gct[:, tile(j)] = dot_t(sel[...], g).astype(BF)

        loop(NT, left_stat)

        def right_stat(j):
            rs_[s, :, tile(j)] = dot(gct[...], gcols(s, j)).astype(BF)

        loop(NT, right_stat)
        put(gmb.at[s], gm_out.at[s], 3 * s)
        put(ls.at[s], sl_out.at[s], 3 * s + 1)
        put(rs_.at[s], sr_out.at[s], 3 * s + 2)

    for s in range(S):
        rcopy(sb.at[s, others(F - 1)], gb.at[s, others(F - 1)], g_s.at[s], g_r.at[s], right).wait_recv()
        selfs[s].wait()

        def halves(j):
            hf[:, tile(j)] = dot(lv[perm[s]], gcols(s, j)).astype(BF)

        loop(NT, halves)

        def mine(j, dn):
            g = dot(sel[...], gcols(s, j))
            gmb[s, :, tile(j)] = g.astype(BF)
            an = av[perm[s], :, tile(j)] + g * g
            dr = g * lax.rsqrt(an)
            return dn + jnp.sum(dr * dr)

        dn = lax.fori_loop(0, NT, mine, jnp.float32(0))

        roots[s][2].wait_recv()
        roots[s][3].wait_recv()

        def weave(t):
            part = [rraw[e, s, pl.ds(pl.multiple_of(t * 16, 16), 16), :].astype(F32) for e in range(4)]
            for h in range(2):
                rows32 = jnp.concatenate([p[8 * h : 8 * h + 8] for p in part], axis=0)
                rn[pl.ds(pl.multiple_of(t * 64 + 32 * h, 32), 32), :] = rows32.astype(BF)

        loop(F // 2, weave)

        def prec(j, pn):
            p = dot(hf[...], rn[:, tile(j)])
            pv[:, tile(j)] = p
            return pn + jnp.sum(p * p)

        pn = lax.fori_loop(0, NT, prec, jnp.float32(0))

        nb[s, d, 0] = jnp.full((8, 128), dn, F32)
        nb[s, d, 1] = jnp.full((8, 128), pn, F32)
        ns = [
            rcopy(nb.at[s, d], nb.at[s, d], n_s.at[s, k], n_r.at[s, k], dev)
            for k, dev in enumerate((right, left, opp))
        ]
        for cp in ns:
            cp.start()
        if s + 1 < S:
            forward_root(s + 1)
            if s + 2 < S:
                start_root(s + 2)
        for cp in ns:
            cp.wait()
        dsum = nb[s, 0, 0] + nb[s, 1, 0] + nb[s, 2, 0] + nb[s, 3, 0]
        psum = nb[s, 0, 1] + nb[s, 1, 1] + nb[s, 2, 1] + nb[s, 3, 1]
        factor = jnp.sqrt(dsum / (psum + 1e-06))[0:1, 0:1]

        def scale(q):
            v = pv[pl.ds(pl.multiple_of(q * 8, 8), 8), :] * factor
            pb[s, q] = jnp.concatenate([v[:, :W2], v[:, W2:]], axis=0).astype(BF)

        loop(F, scale)
        us[s][f] = pb[s, f]

        def send_p(i):
            q = peer(i + 1)
            rcopy(pb.at[s, q], us[s].at[f], p_s.at[s], p_r.at[s], (d, q)).start()

        loop(F - 1, send_p)
        if s >= 1:
            start_third(s - 1)
        statistics(s)
        if s >= 1:
            forward_third(s - 1)

    start_third(S - 1)
    forward_third(S - 1)
    for t in range(S):
        up_copies[t][2].wait_recv()
        up_copies[t][3].wait_recv()
    put(uall, up_out, 3 * S)
    put(tab_v, tab_out, 3 * S + 1)

    for cp in (c1, c2, c3, c4, c5, c6, a1, a2, a3, a4):
        cp.wait_send()
    for s in range(S):
        for cp in up_copies[s]:
            cp.wait_send()
        for cp in roots[s]:
            cp.wait_send()
        rcopy(sb.at[s, others(F - 1)], gb.at[s, others(F - 1)], g_s.at[s], g_r.at[s], right).wait_send()
        rcopy(pb.at[s, others(F - 1)], us[s].at[others(F - 1)], p_s.at[s], p_r.at[s], right).wait_send()
    for cp in out_copies:
        cp.wait()


def finish_kernel(nb, tab, *refs):
    ups, (sl, sr, gm, left, right, acc, up_o, left_o, right_o, acc_o) = refs[:nb], refs[nb:]
    for b in range(nb):
        parts = []
        for e in range(4):
            v = ups[b][e, 0].astype(F32)
            parts.append(jnp.concatenate([v[:8], v[8:]], axis=1))
        up_o[b] = jnp.concatenate(parts, axis=0).astype(BF)
    left_o[...] = 0.95 * left[...] + 0.05 * sl[...].astype(F32)
    right_o[...] = 0.95 * right[...] + 0.05 * sr[...].astype(F32)
    g = gm[...].astype(F32)
    acc_o[...] = acc[...] + g * g


def body(grad_parts, left_stats, right_stats, accum, left_root, right_root, owner_slot):
    N = owner_slot.shape[0]
    F = lax.axis_size("fsdp")
    S = left_stats.shape[0]
    W = left_stats.shape[4]
    SH = F * 8
    H = N // 2
    W2 = W // 2
    hbm = pl.BlockSpec(memory_space=pl.ANY)
    vmem = pl.BlockSpec(memory_space=pltpu.VMEM)
    half = pltpu.VMEM((H, 16, W2), BF)
    whole = pltpu.VMEM((N + 1, 16, W2), BF)
    dma = pltpu.SemaphoreType.DMA
    share = jax.ShapeDtypeStruct((S, SH, W), BF)
    sl, sr, gm, up, tab = pl.pallas_call(
        functools.partial(step_kernel, N, S, F, W),
        out_shape=(share, share, share, jax.ShapeDtypeStruct((4, N, 16, W2), BF),
                   jax.ShapeDtypeStruct((8, 128), jnp.int32)),
        in_specs=[vmem, vmem, hbm, hbm, hbm],
        out_specs=(hbm,) * 5,
        scratch_shapes=[half] * 8
        + [whole] * 4
        + [
            pltpu.VMEM((S, F, 32, W), BF),
            pltpu.VMEM((S, F, 32, W), BF),
            pltpu.VMEM((4, S, SH, W), BF),
            pltpu.VMEM((F * 32, W), BF),
            pltpu.VMEM((S, SH, W), BF),
            pltpu.VMEM((S, SH, W), BF),
            pltpu.VMEM((S, SH, W), F32),
            pltpu.VMEM((SH, F * 32), BF),
            pltpu.VMEM((SH, W), BF),
            pltpu.VMEM((SH, W), F32),
            pltpu.VMEM((SH, F * 32), BF),
            pltpu.VMEM((S, SH, W), BF),
            pltpu.VMEM((S, SH, W), BF),
            pltpu.VMEM((S, SH, W), BF),
            pltpu.VMEM((S, F, 16, W2), BF),
            pltpu.VMEM((F + 1, 16, W2), BF),
            pltpu.VMEM((F + 1, 16, W2), BF),
            pltpu.VMEM((F + 1, 16, W2), BF),
            pltpu.VMEM((4, N, 16, W2), BF),
            pltpu.VMEM((S, 4, 2, 8, 128), F32),
            pltpu.VMEM((8, 128), jnp.int32),
            pltpu.SMEM((8, 128), jnp.int32),
        ]
        + [
            dma((6,)), dma((6,)), dma((4,)), dma((4,)), dma((S, 4)), dma((S, 4)),
            dma((S,)), dma((S,)), dma((S,)), dma((S,)), dma((S, 3)), dma((S, 3)),
            dma((S, 4)), dma((S, 4)), dma((4 + S,)), dma((3 * S + 2,)),
        ],
        compiler_params=pltpu.CompilerParams(
            collective_id=0, has_side_effects=True, vmem_limit_bytes=STEP_VMEM
        ),
        name="shampoo_step",
    )(
        owner_slot[None, :], grad_parts[0],
        left_root.reshape(S, SH, W), right_root.reshape(S, SH, W), accum.reshape(S, SH, W),
    )
    rows = S * SH
    K = 12 if N % 12 == 0 and rows % 12 == 0 and (rows // 12) % 16 == 0 else S
    nb, rb = N // K, rows // K
    per = K // S
    flat = pl.BlockSpec((rb, W), lambda i, tab: (i, 0))
    ranked = pl.BlockSpec((rb, W), lambda i, tab: (tab[3, i // per] * per + i % per, 0))
    picked = [
        pl.BlockSpec((4, 1, 16, W2), lambda i, tab, k=k: (0, tab[4, i * nb + k], 0, 0))
        for k in range(nb)
    ]
    stat = jax.ShapeDtypeStruct((rows, W), F32)
    update, left_out, right_out, accu_out = pl.pallas_call(
        functools.partial(finish_kernel, nb),
        grid_spec=pltpu.PrefetchScalarGridSpec(
            num_scalar_prefetch=1,
            grid=(K,),
            in_specs=picked + [ranked] * 3 + [flat] * 3,
            out_specs=(pl.BlockSpec((nb, 32, W), lambda i, tab: (i, 0, 0)), flat, flat, flat),
        ),
        out_shape=(jax.ShapeDtypeStruct((N, 32, W), BF), stat, stat, stat),
        compiler_params=pltpu.CompilerParams(vmem_limit_bytes=FINISH_VMEM),
        name="shampoo_finish",
    )(
        tab, *([up] * nb), sl.reshape(rows, W), sr.reshape(rows, W), gm.reshape(rows, W),
        left_stats.reshape(rows, W), right_stats.reshape(rows, W), accum.reshape(rows, W),
    )
    layout = left_stats.shape
    return (update, left_out.reshape(layout), right_out.reshape(layout), accu_out.reshape(layout))


def solution(mesh):
    spread = P("fsdp", None, "dp", None, None)
    return jax.shard_map(
        body,
        mesh=mesh,
        in_specs=(P("dp", None, "fsdp", None),) + (spread,) * 5 + (P(),),
        out_specs=(P(None, "fsdp", None), spread, spread, spread),
        check_vma=False,
    )
```

```python
import functools

import jax
import jax.numpy as jnp
from jax import lax
from jax.experimental import pallas as pl
from jax.experimental.pallas import tpu as pltpu
from jax.sharding import PartitionSpec as P

MESH = pl.DeviceIdType.MESH
BF = jnp.bfloat16
F32 = jnp.float32
STEP = 5
STEP_VMEM = 45 << 20
FINISH_VMEM = 18 << 20


def dot(a, b):
    return jnp.dot(a, b, preferred_element_type=F32)


def dot_t(a, b):
    return lax.dot_general(a, b, (((1,), (1,)), ((), ())), preferred_element_type=F32)


def step_kernel(
    N, S, F, W,
    own_ref, gp_in, lr, rr, ac,
    sl_out, sr_out, an_0, an_1, an_2, up_0, up_1, up_2, up_3, nm_out, tab_out,
    gp, ra, rb, fa_raw, fb_raw, ca, cb, fa_comb, fb_comb,
    red_own_0, red_own_1, red_l_0, red_l_1, red_r_0, red_r_1, red_o_0, red_o_1,
    sb, gb, rraw, rn, rv, lv, av, sel, hf, pv, gct, gmb, anb, ls, rs_,
    pb, u_0, u_1, u_2, uall, nb, nl_0, nl_1, nl_2, nall, tab_v, tab,
    rs_s, rs_r, ag_s, ag_r, rt_s, rt_r, g_s, g_r, p_s, p_r, w_s, w_r, n_s, n_r, u_s, u_r, loc, outs,
):
    H = N // 2
    W2, W4 = W // 2, W // 4
    B = F * 32
    SH = F * 8
    T = 256 if W % 256 == 0 else W
    NT = W // T
    nx = 4 if F >= 32 else 2
    nz = F // (2 * nx)
    d = lax.axis_index("dp")
    f = lax.axis_index("fsdp")
    z = f // (2 * nx)
    x = (f // 2) % nx
    c = f % 2
    e1, e2, e3 = lax.rem(d + 1, 4), lax.rem(d + 2, 4), lax.rem(d + 3, 4)
    right, left, opp = (e1, f), (e3, f), (e2, f)
    lo, hi = pl.ds(0, H), pl.ds(H, H)

    def peer(i):
        o = lax.rem(i * STEP, F)
        pz = lax.rem(z + o // (2 * nx), nz)
        px = lax.rem(x + (o // 2) % nx, nx)
        pc = lax.rem(c + o % 2, 2)
        return (pz * nx + px) * 2 + pc

    def rcopy(src, dst, ss, rs, dev):
        return pltpu.make_async_remote_copy(
            src_ref=src, dst_ref=dst, send_sem=ss, recv_sem=rs, device_id=dev, device_id_type=MESH
        )

    def rows(e):
        return pl.ds(pl.multiple_of((e // 2) * 16, 16), 16)

    def cols(e):
        return pl.ds(pl.multiple_of((e % 2) * W2, W2), W2)

    def within(v, top):
        return jnp.minimum(jnp.maximum(v, 0), top)

    def cols4(e, h):
        return pl.ds(pl.multiple_of((e % 2) * W2 + h * W4, W4), W4)

    def part(h):
        return pl.ds(h * W4, W4)

    def loop(n, fn, unroll=1):
        lax.fori_loop(0, n, lambda i, _: (fn(i), 0)[1], 0, unroll=unroll)

    ld_g = pltpu.make_async_copy(gp_in, gp, loc.at[4 + S])
    ld_g.start()
    ld_l = pltpu.make_async_copy(lr, lv, loc.at[0])
    ld_l.start()
    ld_a = pltpu.make_async_copy(ac, av, loc.at[1])
    ld_a.start()
    ld_r = pltpu.make_async_copy(rr, rv, loc.at[2])
    ld_r.start()

    barrier = pltpu.get_barrier_semaphore()

    def greet(i):
        pl.semaphore_signal(barrier, inc=1, device_id=(d, peer(i + 1)), device_id_type=MESH)

    for dev in (right, left, opp):
        pl.semaphore_signal(barrier, inc=1, device_id=dev, device_id_type=MESH)
    loop(F - 1, greet)
    red_own, red_l = (red_own_0, red_own_1), (red_l_0, red_l_1)
    red_r, red_o = (red_r_0, red_r_1), (red_o_0, red_o_1)
    for ref in red_own + red_l + red_r + red_o:
        ref[N] = jnp.zeros((16, W4), BF)
    us = (u_0, u_1, u_2)
    for ref in us:
        ref[F] = jnp.zeros((16, W2), BF)
    nls = (nl_0, nl_1, nl_2)
    for ref in nls:
        ref[F] = jnp.zeros((1, 128), F32)
    pick = lax.broadcasted_iota(jnp.int32, (SH, B), 0)
    at = lax.broadcasted_iota(jnp.int32, (SH, B), 1)
    sel[...] = jnp.where(at == (pick // 8) * 32 + d * 8 + pick % 8, 1.0, 0.0).astype(BF)
    pl.semaphore_wait(barrier, F + 2)

    def tables():
        lanes = 128

        def iota(shape, dim):
            return lax.broadcasted_iota(jnp.int32, shape, dim).astype(F32)

        def count(cond, axis):
            return jnp.sum(jnp.where(cond, 1.0, 0.0), axis=axis, keepdims=True)

        down, along = iota((N, N), 0), iota((N, N), 1)
        own_r = own_ref[...].astype(F32)
        own_rr = jnp.broadcast_to(own_r, (N, N))
        own_c = jnp.sum(jnp.where(down == along, own_rr, 0.0), axis=1, keepdims=True)
        own_cc = jnp.broadcast_to(own_c, (N, N))
        q_r = jnp.floor((own_r + 0.5) * (1.0 / S))
        q_c = jnp.floor((own_c + 0.5) * (1.0 / S))
        same = jnp.broadcast_to(q_c, (N, N)) == jnp.broadcast_to(q_r, (N, N))
        rank_r = count(same & (own_cc < own_rr), 0)
        rank_c = count(same & (own_rr < own_cc), 1)
        rk_r = jnp.broadcast_to(rank_r, (N, N))
        rk_c = jnp.broadcast_to(rank_c, (N, N))
        pos_r = count((rk_c < rk_r) | ((rk_c == rk_r) & (down < along)), 0)
        pos_c = count((rk_r < rk_c) | ((rk_r == rk_c) & (along < down)), 1)
        lane = iota((N, lanes), 1)
        block = iota((N, lanes), 0)
        lane_q = jnp.floor((lane + 0.5) * (1.0 / S))
        lane_r = lane - S * lane_q
        qw = jnp.broadcast_to(q_c, (N, lanes))
        rw = jnp.broadcast_to(rank_c, (N, lanes))
        ow = jnp.broadcast_to(own_c, (N, lanes))
        pw = jnp.broadcast_to(pos_c, (N, lanes))
        inv = jnp.min(
            jnp.where((qw == lane_q) & (rw == lane_r), block, float(N)), axis=0, keepdims=True
        )
        ord_q = jnp.sum(jnp.where(pw == lane, qw, 0.0), axis=0, keepdims=True)
        ord_r = jnp.sum(jnp.where(pw == lane, rw, 0.0), axis=0, keepdims=True)
        base = (f * S).astype(F32)
        here = qw == f.astype(F32)
        total = count(here, 0)
        low = count(here & (ow < base + lane), 0)
        used = count(ow == base + lane, 0)
        rank_s = jnp.where(used > 0.5, low, total + lane[0:1] - low)
        tab_v[0:1, :] = inv.astype(jnp.int32)
        tab_v[1:2, :] = ord_q.astype(jnp.int32)
        tab_v[2:3, :] = ord_r.astype(jnp.int32)
        tab_v[3:4, :] = rank_s.astype(jnp.int32)
        tab_v[4:5, :] = jnp.zeros((1, lanes), jnp.int32)
        tab_v[4:5, 0:N] = pos_r.astype(jnp.int32)
        tab_v[5:8, :] = jnp.zeros((3, lanes), jnp.int32)

    def sums(h):
        p, ss, rs = part(h), rs_s, rs_r
        every_a = (slice(None), slice(None), p)
        return (
            rcopy(gp_in.at[lo, rows(e2), cols4(e2, h)], ra.at[every_a], ss.at[h, 0], rs.at[h, 0], right),
            rcopy(gp_in.at[hi, rows(e2), cols4(e2, h)], rb.at[every_a], ss.at[h, 1], rs.at[h, 1], left),
            rcopy(gp_in.at[hi, rows(e1), cols4(e1, h)], fb_raw.at[every_a], ss.at[h, 2], rs.at[h, 2], right),
            rcopy(gp_in.at[lo, rows(e3), cols4(e3, h)], fa_raw.at[every_a], ss.at[h, 3], rs.at[h, 3], left),
            rcopy(ca.at[every_a], fa_comb.at[every_a], ss.at[h, 4], rs.at[h, 4], right),
            rcopy(cb.at[every_a], fb_comb.at[every_a], ss.at[h, 5], rs.at[h, 5], left),
        )

    def relay(h):
        c, p = halves_of_sum[h], part(h)
        c[0].wait_recv()

        def add_a(b):
            ca[b, :, p] = (ra[b, :, p].astype(F32) + gp[b, rows(e1), cols4(e1, h)].astype(F32)).astype(BF)

        loop(H, add_a)
        c[4].start()
        c[1].wait_recv()

        def add_b(b):
            cb[b, :, p] = (
                rb[b, :, p].astype(F32) + gp[H + b, rows(e3), cols4(e3, h)].astype(F32)
            ).astype(BF)

        loop(H, add_b)
        c[5].start()

    def total(h):
        c, p = halves_of_sum[h], part(h)
        c[3].wait_recv()
        c[4].wait_recv()

        def fin_a(b):
            own = gp[b, rows(d), cols4(d, h)].astype(F32)
            red_own[h][b] = (
                own + fa_raw[b, :, p].astype(F32) + fa_comb[b, :, p].astype(F32)
            ).astype(BF)

        loop(H, fin_a)
        c[2].wait_recv()
        c[5].wait_recv()

        def fin_b(b):
            own = gp[H + b, rows(d), cols4(d, h)].astype(F32)
            red_own[h][H + b] = (
                own + fb_raw[b, :, p].astype(F32) + fb_comb[b, :, p].astype(F32)
            ).astype(BF)

        loop(H, fin_b)

    halves_of_sum = [sums(h) for h in range(2)]
    for k in range(4):
        halves_of_sum[0][k].start()
    tables()
    to_scalars = pltpu.make_async_copy(tab_v, tab, loc.at[3])
    to_scalars.start()
    to_scalars.wait()
    perm = []
    for r in range(S):
        k = jnp.int32(0)
        for s in range(1, S):
            k = jnp.where(tab[3, s] == r, s, k)
        perm.append(within(k, S - 1))
    ld_r.wait()

    def reorder(t):
        part = pl.ds(pl.multiple_of(t * 16, 16), 16)
        for r in range(S):
            rraw[d, r, part, :] = rv[perm[r], part, :]

    loop(SH // 16, reorder)

    every = pl.ds(0, N)

    def gathers(h):
        return (
            rcopy(red_own[h].at[every], red_l[h].at[every], ag_s.at[h, 0], ag_r.at[h, 0], right),
            rcopy(red_own[h].at[every], red_r[h].at[every], ag_s.at[h, 1], ag_r.at[h, 1], left),
            rcopy(red_l[h].at[lo], red_o[h].at[lo], ag_s.at[h, 2], ag_r.at[h, 2], right),
            rcopy(red_r[h].at[hi], red_o[h].at[hi], ag_s.at[h, 3], ag_r.at[h, 3], left),
        )

    sum_gathers = [gathers(h) for h in range(2)]

    def start_gather(h):
        sum_gathers[h][0].start()
        sum_gathers[h][1].start()

    def forward_gather(h):
        sum_gathers[h][0].wait_recv()
        sum_gathers[h][2].start()
        sum_gathers[h][1].wait_recv()
        sum_gathers[h][3].start()

    HR = SH // 2
    up_, dn_ = pl.ds(0, HR), pl.ds(HR, HR)

    def root(s):
        return (
            rcopy(rraw.at[d, s], rraw.at[d, s], rt_s.at[s, 0], rt_r.at[s, 0], right),
            rcopy(rraw.at[d, s], rraw.at[d, s], rt_s.at[s, 1], rt_r.at[s, 1], left),
            rcopy(rraw.at[e3, s, up_], rraw.at[e3, s, up_], rt_s.at[s, 2], rt_r.at[s, 2], right),
            rcopy(rraw.at[e1, s, dn_], rraw.at[e1, s, dn_], rt_s.at[s, 3], rt_r.at[s, 3], left),
        )

    roots = [root(s) for s in range(S)]

    def start_root(s):
        roots[s][0].start()
        roots[s][1].start()

    def forward_root(s):
        roots[s][0].wait_recv()
        roots[s][2].start()
        roots[s][1].wait_recv()
        roots[s][3].start()

    def place(red, e, h):
        def one(q):
            for s in range(S):
                sb[s, q, rows(e), cols4(e, h)] = red[h][within(tab[0, q * S + s], N)]

        loop(F, one)

    def send_eighth(e, h):
        def one(i):
            q = peer(i + 1)
            rcopy(
                sb.at[:, q, rows(e), cols4(e, h)],
                gb.at[:, f, rows(e), cols4(e, h)],
                g_s.at[S], g_r.at[S], (d, q),
            ).start()

        loop(F - 1, one)

    def send_rest(s):
        def one(i):
            q = peer(i + 1)
            for r, c in ((rows(e3), cols4(e3, 1)), (rows(e1), cols4(e1, 1)), (rows(e2), cols(e2))):
                rcopy(sb.at[s, q, r, c], gb.at[s, f, r, c], g_s.at[s], g_r.at[s], (d, q)).start()

        loop(F - 1, one)

    def others(n):
        return pl.ds(0, n)

    ahead = rcopy(
        sb.at[:, others(F - 1), pl.ds(0, 16), :], gb.at[:, others(F - 1), pl.ds(0, 16), :],
        g_s.at[S], g_r.at[S], right,
    )
    rests = [
        rcopy(
            sb.at[s, others(F - 1), pl.ds(0, 16), :], gb.at[s, others(F - 1), pl.ds(0, 16), :],
            g_s.at[s], g_r.at[s], right,
        )
        for s in range(S)
    ]

    ld_g.wait()
    relay(0)
    for k in range(4):
        halves_of_sum[1][k].start()
    total(0)
    start_gather(0)
    place(red_own, d, 0)
    send_eighth(d, 0)
    relay(1)
    total(1)
    start_gather(1)
    place(red_own, d, 1)
    send_eighth(d, 1)
    forward_gather(0)
    place(red_l, e3, 0)
    send_eighth(e3, 0)
    place(red_r, e1, 0)
    send_eighth(e1, 0)
    forward_gather(1)
    start_root(0)
    start_root(1)
    place(red_l, e3, 1)
    place(red_r, e1, 1)
    for h in range(2):
        sum_gathers[h][2].wait_recv()
        sum_gathers[h][3].wait_recv()
        place(red_o, e2, h)
    selfs = [pltpu.make_async_copy(sb.at[s, f], gb.at[s, f], loc.at[4 + s]) for s in range(S)]
    send_rest(0)
    for s in range(S):
        selfs[s].start()
    send_rest(1)
    forward_root(0)
    start_root(2)
    ld_l.wait()
    ld_a.wait()

    def tile(j):
        return pl.ds(pl.multiple_of(j * T, T), T)

    def gcols(s, j):
        return gb[s, :, :, tile(j)].reshape(B, T)

    def grows(s, j):
        return gb[s, pl.ds(j * (T // 32), T // 32)].reshape(T, W)

    out_copies = {}

    def put(src, dst, k, s):
        cp = pltpu.make_async_copy(src, dst, outs.at[k, s])
        cp.start()
        out_copies[id(src)] = cp

    def free(src):
        cp = out_copies.pop(id(src), None)
        if cp is not None:
            cp.wait()

    def third(t):
        n = N // S
        own = pl.ds(t * n, n)
        a, b = pl.ds(t * n, n // 2), pl.ds(t * n + n // 2, n - n // 2)
        return (
            rcopy(uall.at[d, own], uall.at[d, own], u_s.at[t, 0], u_r.at[t, 0], right),
            rcopy(uall.at[d, own], uall.at[d, own], u_s.at[t, 1], u_r.at[t, 1], left),
            rcopy(uall.at[e3, a], uall.at[e3, a], u_s.at[t, 2], u_r.at[t, 2], right),
            rcopy(uall.at[e1, b], uall.at[e1, b], u_s.at[t, 3], u_r.at[t, 3], left),
        ) + tuple(
            rcopy(nall.at[d, own], nall.at[d, own], n_s.at[t, k], n_r.at[t, k], dev)
            for k, dev in enumerate((right, left, opp))
        )

    up_copies = [third(t) for t in range(S)]

    def shares(t):
        return rcopy(
            nls[t].at[others(F - 1)], nls[t].at[others(F - 1)], w_s.at[t], w_r.at[t], right
        )

    def start_third(t):
        rcopy(
            pb.at[t, others(F - 1)], us[t].at[others(F - 1)], p_s.at[t], p_r.at[t], right
        ).wait_recv()
        shares(t).wait_recv()

        def choose(i):
            j = t * (N // S) + i
            q, r = within(tab[1, j], F), tab[2, j]
            v = us[0][jnp.where(r == 0, q, F)].astype(F32)
            n = nls[0][jnp.where(r == 0, q, F)]
            for k in range(1, t + 1):
                v = v + us[k][jnp.where(r == k, q, F)].astype(F32)
                n = n + nls[k][jnp.where(r == k, q, F)]
            uall[d, j] = v.astype(BF)
            nall[d, j] = n

        loop(N // S, choose)
        for k in (0, 1, 4, 5, 6):
            up_copies[t][k].start()

    def forward_third(t):
        up_copies[t][0].wait_recv()
        up_copies[t][2].start()
        up_copies[t][1].wait_recv()
        up_copies[t][3].start()

    def statistics(s):
        free(ls)
        free(rs_)

        def left_stat(j):
            g = grows(s, j)
            ls[:, tile(j)] = dot_t(gmb[...], g).astype(BF)
            gct[:, tile(j)] = dot_t(sel[...], g).astype(BF)

        loop(NT, left_stat)
        put(ls, sl_out.at[s], 1, s)

        def right_stat(j):
            rs_[:, tile(j)] = dot(gct[...], gcols(s, j)).astype(BF)

        loop(NT, right_stat)
        put(rs_, sr_out.at[s], 2, s)

    def land_third(t):
        for k in (2, 3, 4, 5, 6):
            up_copies[t][k].wait_recv()
        own = pl.ds(t * (N // S), N // S)
        pairs = [(uall.at[e, own], up.at[own]) for e, up in enumerate((up_0, up_1, up_2, up_3))]
        for k, (src, dst) in enumerate(pairs + [(nall.at[:, own], nm_out.at[:, own])]):
            cp = pltpu.make_async_copy(src, dst, outs.at[4 + k, t])
            cp.start()
            landed.append(cp)

    landed = []
    tab_copy = pltpu.make_async_copy(tab_v, tab_out, outs.at[3, 0])
    tab_copy.start()
    ahead.wait_recv()
    for s in range(S):
        rests[s].wait_recv()
        selfs[s].wait()

        def halves(j):
            hf[:, tile(j)] = dot(lv[perm[s]], gcols(s, j)).astype(BF)

        loop(NT, halves)

        def mine(j, dn):
            g = dot(sel[...], gcols(s, j))
            gmb[:, tile(j)] = g.astype(BF)
            an = av[perm[s], :, tile(j)] + g * g
            anb[:, tile(j)] = an
            dr = g * lax.rsqrt(an)
            return dn + jnp.sum(dr * dr)

        free(anb)
        dn = lax.fori_loop(0, NT, mine, jnp.float32(0))
        put(anb, (an_0, an_1, an_2)[s], 0, s)

        if s + 1 < S:
            forward_root(s + 1)
        else:
            forward_third(0)
            statistics(s)
        roots[s][2].wait_recv()
        roots[s][3].wait_recv()

        def weave(t):
            part16 = pl.ds(pl.multiple_of(t * 16, 16), 16)
            quarter = [rraw[e, s, part16, :].astype(F32) for e in range(4)]
            for h in range(2):
                rows32 = jnp.concatenate([p[8 * h : 8 * h + 8] for p in quarter], axis=0)
                rn[pl.ds(pl.multiple_of(t * 64 + 32 * h, 32), 32), :] = rows32.astype(BF)

        loop(F // 2, weave)

        def prec(j, pn):
            p = dot(hf[...], rn[:, tile(j)])
            pv[:, tile(j)] = p
            return pn + jnp.sum(p * p)

        pn = lax.fori_loop(0, NT, prec, jnp.float32(0))

        lane = lax.broadcasted_iota(jnp.int32, (1, 128), 1)
        nb[s] = jnp.where(lane == 0, dn, jnp.where(lane == 1, pn, 0.0))

        def pack(q):
            v = pv[pl.ds(pl.multiple_of(q * 8, 8), 8), :]
            pb[s, q] = jnp.concatenate([v[:, :W2], v[:, W2:]], axis=0).astype(BF)

        loop(F, pack)
        us[s][f] = pb[s, f]
        nls[s][f] = nb[s]

        def send_p(i):
            q = peer(i + 1)
            rcopy(pb.at[s, q], us[s].at[f], p_s.at[s], p_r.at[s], (d, q)).start()
            rcopy(nb.at[s], nls[s].at[f], w_s.at[s], w_r.at[s], (d, q)).start()

        loop(F - 1, send_p)
        if s == 0:
            send_rest(2)
        if s == 1:
            start_third(0)
        if s + 1 < S:
            statistics(s)
        else:
            start_third(1)

    land_third(0)
    forward_third(1)
    start_third(2)
    land_third(1)
    forward_third(2)
    land_third(2)
    for h in range(2):
        for cp in halves_of_sum[h] + sum_gathers[h]:
            cp.wait_send()
    ahead.wait_send()
    for s in range(S):
        for cp in up_copies[s]:
            cp.wait_send()
        for cp in roots[s]:
            cp.wait_send()
        rests[s].wait_send()
        shares(s).wait_send()
        rcopy(pb.at[s, others(F - 1)], us[s].at[others(F - 1)], p_s.at[s], p_r.at[s], right).wait_send()
    for cp in landed + [tab_copy] + list(out_copies.values()):
        cp.wait()


def finish_kernel(nb, per, tab, *refs):
    ups, (nm, a0, a1, a2, sl, sr, left, right, up_o, left_o, right_o, acc_o) = refs[:4], refs[4:]
    step = pl.program_id(0)
    for b in range(nb):
        at = tab[4, step * nb + b]
        norms = nm[0, at] + nm[1, at] + nm[2, at] + nm[3, at]
        factor = jnp.sqrt(norms[:, 0:1] / (norms[:, 1:2] + 1e-06))
        parts = []
        for e in range(4):
            v = ups[e][at].astype(F32) * factor
            parts.append(jnp.concatenate([v[:8], v[8:]], axis=1))
        up_o[b] = jnp.concatenate(parts, axis=0).astype(BF)
    rank = jnp.full(acc_o.shape, tab[3, step // per], jnp.int32)
    acc_o[...] = jnp.where(rank == 0, a0[...], jnp.where(rank == 1, a1[...], a2[...]))
    left_o[...] = 0.95 * left[...] + 0.05 * sl[...].astype(F32)
    right_o[...] = 0.95 * right[...] + 0.05 * sr[...].astype(F32)


def body(grad_parts, left_stats, right_stats, accum, left_root, right_root, owner_slot):
    N = owner_slot.shape[0]
    F = lax.axis_size("fsdp")
    S = left_stats.shape[0]
    W = left_stats.shape[4]
    SH = F * 8
    H = N // 2
    W2 = W // 2
    hbm = pl.BlockSpec(memory_space=pl.ANY)
    vmem = pl.BlockSpec(memory_space=pltpu.VMEM)
    half = pltpu.VMEM((H, 16, W2), BF)
    whole = pltpu.VMEM((N + 1, 16, W // 4), BF)
    dma = pltpu.SemaphoreType.DMA
    share = jax.ShapeDtypeStruct((S, SH, W), BF)
    sl, sr, a0, a1, a2, up0, up1, up2, up3, nm, tab = pl.pallas_call(
        functools.partial(step_kernel, N, S, F, W),
        out_shape=(share, share) + (jax.ShapeDtypeStruct((SH, W), F32),) * 3
                  + (jax.ShapeDtypeStruct((N, 16, W2), BF),) * 4 + (
                   jax.ShapeDtypeStruct((4, N, 1, 128), F32),
                   jax.ShapeDtypeStruct((8, 128), jnp.int32)),
        in_specs=[vmem, hbm, hbm, hbm, hbm],
        out_specs=(hbm,) * 11,
        scratch_shapes=[pltpu.VMEM((N, 32, W), BF)]
        + [half] * 8
        + [whole] * 8
        + [
            pltpu.VMEM((S, F, 32, W), BF),
            pltpu.VMEM((S, F, 32, W), BF),
            pltpu.VMEM((4, S, SH, W), BF),
            pltpu.VMEM((F * 32, W), BF),
            pltpu.VMEM((S, SH, W), BF),
            pltpu.VMEM((S, SH, W), BF),
            pltpu.VMEM((S, SH, W), F32),
            pltpu.VMEM((SH, F * 32), BF),
            pltpu.VMEM((SH, W), BF),
            pltpu.VMEM((SH, W), F32),
            pltpu.VMEM((SH, F * 32), BF),
            pltpu.VMEM((SH, W), BF),
            pltpu.VMEM((SH, W), F32),
            pltpu.VMEM((SH, W), BF),
            pltpu.VMEM((SH, W), BF),
            pltpu.VMEM((S, F, 16, W2), BF),
            pltpu.VMEM((F + 1, 16, W2), BF),
            pltpu.VMEM((F + 1, 16, W2), BF),
            pltpu.VMEM((F + 1, 16, W2), BF),
            pltpu.VMEM((4, N, 16, W2), BF),
            pltpu.VMEM((S, 1, 128), F32),
            pltpu.VMEM((F + 1, 1, 128), F32),
            pltpu.VMEM((F + 1, 1, 128), F32),
            pltpu.VMEM((F + 1, 1, 128), F32),
            pltpu.VMEM((4, N, 1, 128), F32),
            pltpu.VMEM((8, 128), jnp.int32),
            pltpu.SMEM((8, 128), jnp.int32),
        ]
        + [
            dma((2, 6)), dma((2, 6)), dma((2, 4)), dma((2, 4)), dma((S, 4)), dma((S, 4)),
            dma((S + 1,)), dma((S + 1,)), dma((S,)), dma((S,)), dma((S,)), dma((S,)), dma((S, 3)), dma((S, 3)),
            dma((S, 4)), dma((S, 4)), dma((5 + S,)), dma((9, S)),
        ],
        compiler_params=pltpu.CompilerParams(
            collective_id=0, has_side_effects=True, vmem_limit_bytes=STEP_VMEM
        ),
        name="shampoo_step",
    )(
        owner_slot[None, :], grad_parts[0],
        left_root.reshape(S, SH, W), right_root.reshape(S, SH, W), accum.reshape(S, SH, W),
    )
    rows = S * SH
    K = 2 * S if N % (2 * S) == 0 and (rows // (2 * S)) % 16 == 0 else S
    nb, rb = N // K, rows // K
    per = K // S
    flat = pl.BlockSpec((rb, W), lambda i, tab: (i, 0))
    ranked = pl.BlockSpec((rb, W), lambda i, tab: (tab[3, i // per] * per + i % per, 0))
    one_rank = pl.BlockSpec((rb, W), lambda i, tab: (i % per, 0))

    def full(shape):
        return pl.BlockSpec(shape, lambda i, tab: (0,) * len(shape))

    stat = jax.ShapeDtypeStruct((rows, W), F32)
    update, left_out, right_out, accu_out = pl.pallas_call(
        functools.partial(finish_kernel, nb, per),
        grid_spec=pltpu.PrefetchScalarGridSpec(
            num_scalar_prefetch=1,
            grid=(K,),
            in_specs=[full((N, 16, W2))] * 4
            + [full((4, N, 1, 128))]
            + [one_rank] * 3
            + [ranked] * 2
            + [flat] * 2,
            out_specs=(pl.BlockSpec((nb, 32, W), lambda i, tab: (i, 0, 0)), flat, flat, flat),
        ),
        out_shape=(jax.ShapeDtypeStruct((N, 32, W), BF), stat, stat, stat),
        compiler_params=pltpu.CompilerParams(vmem_limit_bytes=FINISH_VMEM),
        name="shampoo_finish",
    )(
        tab, up0, up1, up2, up3, nm, a0, a1, a2, sl.reshape(rows, W), sr.reshape(rows, W),
        left_stats.reshape(rows, W), right_stats.reshape(rows, W),
    )
    layout = left_stats.shape
    return (update, left_out.reshape(layout), right_out.reshape(layout), accu_out.reshape(layout))


def solution(mesh):
    spread = P("fsdp", None, "dp", None, None)
    return jax.shard_map(
        body,
        mesh=mesh,
        in_specs=(P("dp", None, "fsdp", None),) + (spread,) * 5 + (P(),),
        out_specs=(P(None, "fsdp", None), spread, spread, spread),
        check_vma=False,
    )
```

```python
import functools

import jax
import jax.numpy as jnp
from jax import lax
from jax.experimental import pallas as pl
from jax.experimental.pallas import tpu as pltpu
from jax.sharding import PartitionSpec as P

MESH = pl.DeviceIdType.MESH
BF = jnp.bfloat16
F32 = jnp.float32
STEP = 5
STEP_VMEM = 45 << 20
FINISH_VMEM = 18 << 20


def dot(a, b):
    return jnp.dot(a, b, preferred_element_type=F32)


def dot_t(a, b):
    return lax.dot_general(a, b, (((1,), (1,)), ((), ())), preferred_element_type=F32)


def step_kernel(
    N, S, F, W,
    own_ref, gp_in, lr, rr, ac,
    sl_out, sr_out, an_0, an_1, an_2, up_0, up_1, up_2, up_3, nm_out, tab_out,
    gp, ra, rb, fa_raw, fb_raw, ca, cb, fa_comb, fb_comb,
    red_own_0, red_own_1, red_l_0, red_l_1, red_r_0, red_r_1, red_o_0, red_o_1,
    sb, gb, rraw, rn, rv, lv, av, sel, hf, pv, gct, gmb, anb, ls, rs_,
    pb, u_0, u_1, u_2, uall, nb, nl_0, nl_1, nl_2, nall, tab_v, tab,
    rs_s, rs_r, ag_s, ag_r, rt_s, rt_r, g_s, g_r, p_s, p_r, w_s, w_r, n_s, n_r, u_s, u_r, loc, outs,
):
    H = N // 2
    W2, W4 = W // 2, W // 4
    B = F * 32
    SH = F * 8
    T = 256 if W % 256 == 0 else W
    NT = W // T
    nx = 4 if F >= 32 else 2
    nz = F // (2 * nx)
    d = lax.axis_index("dp")
    f = lax.axis_index("fsdp")
    z = f // (2 * nx)
    x = (f // 2) % nx
    c = f % 2
    e1, e2, e3 = lax.rem(d + 1, 4), lax.rem(d + 2, 4), lax.rem(d + 3, 4)
    right, left, opp = (e1, f), (e3, f), (e2, f)
    lo, hi = pl.ds(0, H), pl.ds(H, H)

    def peer(i):
        o = lax.rem(i * STEP, F)
        pz = lax.rem(z + o // (2 * nx), nz)
        px = lax.rem(x + (o // 2) % nx, nx)
        pc = lax.rem(c + o % 2, 2)
        return (pz * nx + px) * 2 + pc

    def rcopy(src, dst, ss, rs, dev):
        return pltpu.make_async_remote_copy(
            src_ref=src, dst_ref=dst, send_sem=ss, recv_sem=rs, device_id=dev, device_id_type=MESH
        )

    def rows(e):
        return pl.ds(pl.multiple_of((e // 2) * 16, 16), 16)

    def cols(e):
        return pl.ds(pl.multiple_of((e % 2) * W2, W2), W2)

    def within(v, top):
        return jnp.minimum(jnp.maximum(v, 0), top)

    def cols4(e, h):
        return pl.ds(pl.multiple_of((e % 2) * W2 + h * W4, W4), W4)

    def part(h):
        return pl.ds(h * W4, W4)

    def loop(n, fn, unroll=4):
        unroll = n if n == F - 1 else unroll
        unroll = unroll if n % unroll == 0 else 1
        lax.fori_loop(0, n, lambda i, _: (fn(i), 0)[1], 0, unroll=unroll)

    ld_g = pltpu.make_async_copy(gp_in, gp, loc.at[4 + S])
    ld_g.start()
    ld_l = pltpu.make_async_copy(lr, lv, loc.at[0])
    ld_l.start()
    ld_a = pltpu.make_async_copy(ac, av, loc.at[1])
    ld_a.start()
    ld_r = pltpu.make_async_copy(rr, rv, loc.at[2])
    ld_r.start()

    barrier = pltpu.get_barrier_semaphore()

    def greet(i):
        pl.semaphore_signal(barrier, inc=1, device_id=(d, peer(i + 1)), device_id_type=MESH)

    for dev in (right, left, opp):
        pl.semaphore_signal(barrier, inc=1, device_id=dev, device_id_type=MESH)
    loop(F - 1, greet)
    red_own, red_l = (red_own_0, red_own_1), (red_l_0, red_l_1)
    red_r, red_o = (red_r_0, red_r_1), (red_o_0, red_o_1)
    pl.semaphore_wait(barrier, F + 2)

    def tables():
        lanes = 128

        def iota(shape, dim):
            return lax.broadcasted_iota(jnp.int32, shape, dim).astype(F32)

        def count(cond, axis):
            return jnp.sum(jnp.where(cond, 1.0, 0.0), axis=axis, keepdims=True)

        down, along = iota((N, N), 0), iota((N, N), 1)
        own_r = own_ref[...].astype(F32)
        own_rr = jnp.broadcast_to(own_r, (N, N))
        own_c = jnp.sum(jnp.where(down == along, own_rr, 0.0), axis=1, keepdims=True)
        own_cc = jnp.broadcast_to(own_c, (N, N))
        q_r = jnp.floor((own_r + 0.5) * (1.0 / S))
        q_c = jnp.floor((own_c + 0.5) * (1.0 / S))
        same = jnp.broadcast_to(q_c, (N, N)) == jnp.broadcast_to(q_r, (N, N))
        rank_r = count(same & (own_cc < own_rr), 0)
        rank_c = count(same & (own_rr < own_cc), 1)
        rk_r = jnp.broadcast_to(rank_r, (N, N))
        rk_c = jnp.broadcast_to(rank_c, (N, N))
        pos_r = count((rk_c < rk_r) | ((rk_c == rk_r) & (down < along)), 0)
        pos_c = count((rk_r < rk_c) | ((rk_r == rk_c) & (along < down)), 1)
        lane = iota((N, lanes), 1)
        block = iota((N, lanes), 0)
        lane_q = jnp.floor((lane + 0.5) * (1.0 / S))
        lane_r = lane - S * lane_q
        qw = jnp.broadcast_to(q_c, (N, lanes))
        rw = jnp.broadcast_to(rank_c, (N, lanes))
        ow = jnp.broadcast_to(own_c, (N, lanes))
        pw = jnp.broadcast_to(pos_c, (N, lanes))
        inv = jnp.min(
            jnp.where((qw == lane_q) & (rw == lane_r), block, float(N)), axis=0, keepdims=True
        )
        ord_q = jnp.sum(jnp.where(pw == lane, qw, 0.0), axis=0, keepdims=True)
        ord_r = jnp.sum(jnp.where(pw == lane, rw, 0.0), axis=0, keepdims=True)
        base = (f * S).astype(F32)
        here = qw == f.astype(F32)
        total = count(here, 0)
        low = count(here & (ow < base + lane), 0)
        used = count(ow == base + lane, 0)
        rank_s = jnp.where(used > 0.5, low, total + lane[0:1] - low)
        tab_v[0:1, :] = inv.astype(jnp.int32)
        tab_v[1:2, :] = ord_q.astype(jnp.int32)
        tab_v[2:3, :] = ord_r.astype(jnp.int32)
        tab_v[3:4, :] = rank_s.astype(jnp.int32)
        tab_v[4:5, :] = jnp.zeros((1, lanes), jnp.int32)
        tab_v[4:5, 0:N] = pos_r.astype(jnp.int32)
        tab_v[5:8, :] = jnp.zeros((3, lanes), jnp.int32)

    def sums(h):
        p, ss, rs = part(h), rs_s, rs_r
        every_a = (slice(None), slice(None), p)
        return (
            rcopy(gp_in.at[lo, rows(e2), cols4(e2, h)], ra.at[every_a], ss.at[h, 0], rs.at[h, 0], right),
            rcopy(gp_in.at[hi, rows(e2), cols4(e2, h)], rb.at[every_a], ss.at[h, 1], rs.at[h, 1], left),
            rcopy(gp_in.at[hi, rows(e1), cols4(e1, h)], fb_raw.at[every_a], ss.at[h, 2], rs.at[h, 2], right),
            rcopy(gp_in.at[lo, rows(e3), cols4(e3, h)], fa_raw.at[every_a], ss.at[h, 3], rs.at[h, 3], left),
            rcopy(ca.at[every_a], fa_comb.at[every_a], ss.at[h, 4], rs.at[h, 4], right),
            rcopy(cb.at[every_a], fb_comb.at[every_a], ss.at[h, 5], rs.at[h, 5], left),
        )

    def relay(h):
        c, p = halves_of_sum[h], part(h)
        c[0].wait_recv()

        def add_a(b):
            ca[b, :, p] = (ra[b, :, p].astype(F32) + gp[b, rows(e1), cols4(e1, h)].astype(F32)).astype(BF)

        loop(H, add_a, 3)
        c[4].start()
        c[1].wait_recv()

        def add_b(b):
            cb[b, :, p] = (
                rb[b, :, p].astype(F32) + gp[H + b, rows(e3), cols4(e3, h)].astype(F32)
            ).astype(BF)

        loop(H, add_b, 3)
        c[5].start()

    def total(h):
        c, p = halves_of_sum[h], part(h)
        c[3].wait_recv()
        c[4].wait_recv()

        def fin_a(b):
            own = gp[b, rows(d), cols4(d, h)].astype(F32)
            red_own[h][b] = (
                own + fa_raw[b, :, p].astype(F32) + fa_comb[b, :, p].astype(F32)
            ).astype(BF)

        loop(H, fin_a, 3)
        c[2].wait_recv()
        c[5].wait_recv()

        def fin_b(b):
            own = gp[H + b, rows(d), cols4(d, h)].astype(F32)
            red_own[h][H + b] = (
                own + fb_raw[b, :, p].astype(F32) + fb_comb[b, :, p].astype(F32)
            ).astype(BF)

        loop(H, fin_b, 3)

    halves_of_sum = [sums(h) for h in range(2)]
    for k in range(4):
        halves_of_sum[0][k].start()

    every = pl.ds(0, N)

    def gathers(h):
        return (
            rcopy(red_own[h].at[every], red_l[h].at[every], ag_s.at[h, 0], ag_r.at[h, 0], right),
            rcopy(red_own[h].at[every], red_r[h].at[every], ag_s.at[h, 1], ag_r.at[h, 1], left),
            rcopy(red_l[h].at[lo], red_o[h].at[lo], ag_s.at[h, 2], ag_r.at[h, 2], right),
            rcopy(red_r[h].at[hi], red_o[h].at[hi], ag_s.at[h, 3], ag_r.at[h, 3], left),
        )

    sum_gathers = [gathers(h) for h in range(2)]

    def start_gather(h):
        sum_gathers[h][0].start()
        sum_gathers[h][1].start()

    def forward_gather(h):
        sum_gathers[h][0].wait_recv()
        sum_gathers[h][2].start()
        sum_gathers[h][1].wait_recv()
        sum_gathers[h][3].start()

    HR = SH // 2
    up_, dn_ = pl.ds(0, HR), pl.ds(HR, HR)

    def root(s):
        return (
            rcopy(rraw.at[d, s], rraw.at[d, s], rt_s.at[s, 0], rt_r.at[s, 0], right),
            rcopy(rraw.at[d, s], rraw.at[d, s], rt_s.at[s, 1], rt_r.at[s, 1], left),
            rcopy(rraw.at[e3, s, up_], rraw.at[e3, s, up_], rt_s.at[s, 2], rt_r.at[s, 2], right),
            rcopy(rraw.at[e1, s, dn_], rraw.at[e1, s, dn_], rt_s.at[s, 3], rt_r.at[s, 3], left),
        )

    roots = [root(s) for s in range(S)]

    def start_root(s):
        roots[s][0].start()
        roots[s][1].start()

    def forward_root(s):
        roots[s][0].wait_recv()
        roots[s][2].start()
        roots[s][1].wait_recv()
        roots[s][3].start()

    def place(red, e, h):
        def one(q):
            for s in range(S):
                sb[s, q, rows(e), cols4(e, h)] = red[h][within(tab[0, q * S + s], N)]

        loop(F, one)

    def send_eighth(e, h):
        def one(i):
            q = peer(i + 1)
            rcopy(
                sb.at[:, q, rows(e), cols4(e, h)],
                gb.at[:, f, rows(e), cols4(e, h)],
                g_s.at[S], g_r.at[S], (d, q),
            ).start()

        loop(F - 1, one)

    def send_rest(s):
        def one(i):
            q = peer(i + 1)
            for r, c in ((rows(e3), cols4(e3, 1)), (rows(e1), cols4(e1, 1)), (rows(e2), cols(e2))):
                rcopy(sb.at[s, q, r, c], gb.at[s, f, r, c], g_s.at[s], g_r.at[s], (d, q)).start()

        loop(F - 1, one)

    def others(n):
        return pl.ds(0, n)

    ahead = rcopy(
        sb.at[:, others(F - 1), pl.ds(0, 16), :], gb.at[:, others(F - 1), pl.ds(0, 16), :],
        g_s.at[S], g_r.at[S], right,
    )
    rests = [
        rcopy(
            sb.at[s, others(F - 1), pl.ds(0, 16), :], gb.at[s, others(F - 1), pl.ds(0, 16), :],
            g_s.at[s], g_r.at[s], right,
        )
        for s in range(S)
    ]

    ld_g.wait()
    relay(0)
    for k in range(4):
        halves_of_sum[1][k].start()
    for ref in red_own + red_l + red_r + red_o:
        ref[N] = jnp.zeros((16, W4), BF)
    us = (u_0, u_1, u_2)
    for ref in us:
        ref[F] = jnp.zeros((16, W2), BF)
    nls = (nl_0, nl_1, nl_2)
    for ref in nls:
        ref[F] = jnp.zeros((1, 128), F32)
    pick = lax.broadcasted_iota(jnp.int32, (SH, B), 0)
    at = lax.broadcasted_iota(jnp.int32, (SH, B), 1)
    sel[...] = jnp.where(at == (pick // 8) * 32 + d * 8 + pick % 8, 1.0, 0.0).astype(BF)
    tables()
    to_scalars = pltpu.make_async_copy(tab_v, tab, loc.at[3])
    to_scalars.start()
    to_scalars.wait()
    perm = []
    for r in range(S):
        k = jnp.int32(0)
        for s in range(1, S):
            k = jnp.where(tab[3, s] == r, s, k)
        perm.append(within(k, S - 1))
    total(0)
    start_gather(0)
    place(red_own, d, 0)
    send_eighth(d, 0)
    relay(1)
    total(1)
    start_gather(1)
    place(red_own, d, 1)
    send_eighth(d, 1)
    ld_r.wait()

    def reorder(t):
        part = pl.ds(pl.multiple_of(t * 16, 16), 16)
        for r in range(S):
            rraw[d, r, part, :] = rv[perm[r], part, :]

    loop(SH // 16, reorder)
    forward_gather(0)
    place(red_l, e3, 0)
    send_eighth(e3, 0)
    place(red_r, e1, 0)
    send_eighth(e1, 0)
    forward_gather(1)
    start_root(0)
    start_root(1)
    place(red_l, e3, 1)
    place(red_r, e1, 1)
    for h in range(2):
        sum_gathers[h][2].wait_recv()
        sum_gathers[h][3].wait_recv()
        place(red_o, e2, h)
    selfs = [pltpu.make_async_copy(sb.at[s, f], gb.at[s, f], loc.at[4 + s]) for s in range(S)]
    send_rest(0)
    for s in range(S):
        selfs[s].start()
    send_rest(1)
    forward_root(0)
    start_root(2)
    ld_l.wait()
    ld_a.wait()

    def tile(j):
        return pl.ds(pl.multiple_of(j * T, T), T)

    def gcols(s, j):
        return gb[s, :, :, tile(j)].reshape(B, T)

    def grows(s, j):
        return gb[s, pl.ds(j * (T // 32), T // 32)].reshape(T, W)

    out_copies = {}

    def put(src, dst, k, s):
        cp = pltpu.make_async_copy(src, dst, outs.at[k, s])
        cp.start()
        out_copies[id(src)] = cp

    def free(src):
        cp = out_copies.pop(id(src), None)
        if cp is not None:
            cp.wait()

    def third(t):
        n = N // S
        own = pl.ds(t * n, n)
        a, b = pl.ds(t * n, n // 2), pl.ds(t * n + n // 2, n - n // 2)
        return (
            rcopy(uall.at[d, own], uall.at[d, own], u_s.at[t, 0], u_r.at[t, 0], right),
            rcopy(uall.at[d, own], uall.at[d, own], u_s.at[t, 1], u_r.at[t, 1], left),
            rcopy(uall.at[e3, a], uall.at[e3, a], u_s.at[t, 2], u_r.at[t, 2], right),
            rcopy(uall.at[e1, b], uall.at[e1, b], u_s.at[t, 3], u_r.at[t, 3], left),
        ) + tuple(
            rcopy(nall.at[d, own], nall.at[d, own], n_s.at[t, k], n_r.at[t, k], dev)
            for k, dev in enumerate((right, left, opp))
        )

    up_copies = [third(t) for t in range(S)]

    def shares(t):
        return rcopy(
            nls[t].at[others(F - 1)], nls[t].at[others(F - 1)], w_s.at[t], w_r.at[t], right
        )

    def start_third(t):
        rcopy(
            pb.at[t, others(F - 1)], us[t].at[others(F - 1)], p_s.at[t], p_r.at[t], right
        ).wait_recv()
        shares(t).wait_recv()

        def choose(i):
            j = t * (N // S) + i
            q, r = within(tab[1, j], F), tab[2, j]
            v = us[0][jnp.where(r == 0, q, F)].astype(F32)
            n = nls[0][jnp.where(r == 0, q, F)]
            for k in range(1, t + 1):
                v = v + us[k][jnp.where(r == k, q, F)].astype(F32)
                n = n + nls[k][jnp.where(r == k, q, F)]
            uall[d, j] = v.astype(BF)
            nall[d, j] = n

        loop(N // S, choose)
        for k in (0, 1, 4, 5, 6):
            up_copies[t][k].start()

    def forward_third(t):
        up_copies[t][0].wait_recv()
        up_copies[t][2].start()
        up_copies[t][1].wait_recv()
        up_copies[t][3].start()

    def statistics(s):
        free(ls)
        free(rs_)

        def left_stat(j):
            g = grows(s, j)
            ls[:, tile(j)] = dot_t(gmb[...], g).astype(BF)
            gct[:, tile(j)] = dot_t(sel[...], g).astype(BF)

        loop(NT, left_stat, 1)
        put(ls, sl_out.at[s], 1, s)

        def right_stat(j):
            rs_[:, tile(j)] = dot(gct[...], gcols(s, j)).astype(BF)

        loop(NT, right_stat, 1)
        put(rs_, sr_out.at[s], 2, s)

    def land_third(t):
        for k in (2, 3, 4, 5, 6):
            up_copies[t][k].wait_recv()
        own = pl.ds(t * (N // S), N // S)
        pairs = [(uall.at[e, own], up.at[own]) for e, up in enumerate((up_0, up_1, up_2, up_3))]
        for k, (src, dst) in enumerate(pairs + [(nall.at[:, own], nm_out.at[:, own])]):
            cp = pltpu.make_async_copy(src, dst, outs.at[4 + k, t])
            cp.start()
            landed.append(cp)

    landed = []
    tab_copy = pltpu.make_async_copy(tab_v, tab_out, outs.at[3, 0])
    tab_copy.start()
    ahead.wait_recv()
    for s in range(S):
        rests[s].wait_recv()
        selfs[s].wait()

        def halves(j):
            hf[:, tile(j)] = dot(lv[perm[s]], gcols(s, j)).astype(BF)

        loop(NT, halves, 1)

        def mine(j, dn):
            g = dot(sel[...], gcols(s, j))
            gmb[:, tile(j)] = g.astype(BF)
            an = av[perm[s], :, tile(j)] + g * g
            anb[:, tile(j)] = an
            dr = g * lax.rsqrt(an)
            return dn + jnp.sum(dr * dr)

        free(anb)
        dn = lax.fori_loop(0, NT, mine, jnp.float32(0))
        put(anb, (an_0, an_1, an_2)[s], 0, s)

        if s + 1 < S:
            forward_root(s + 1)
        else:
            forward_third(0)
            statistics(s)
        roots[s][2].wait_recv()
        roots[s][3].wait_recv()

        def weave(t):
            part16 = pl.ds(pl.multiple_of(t * 16, 16), 16)
            quarter = [rraw[e, s, part16, :].astype(F32) for e in range(4)]
            for h in range(2):
                rows32 = jnp.concatenate([p[8 * h : 8 * h + 8] for p in quarter], axis=0)
                rn[pl.ds(pl.multiple_of(t * 64 + 32 * h, 32), 32), :] = rows32.astype(BF)

        loop(F // 2, weave)

        def prec(j, pn):
            p = dot(hf[...], rn[:, tile(j)])
            pv[:, tile(j)] = p
            return pn + jnp.sum(p * p)

        pn = lax.fori_loop(0, NT, prec, jnp.float32(0))

        lane = lax.broadcasted_iota(jnp.int32, (1, 128), 1)
        nb[s] = jnp.where(lane == 0, dn, jnp.where(lane == 1, pn, 0.0))

        def pack(q):
            v = pv[pl.ds(pl.multiple_of(q * 8, 8), 8), :]
            pb[s, q] = jnp.concatenate([v[:, :W2], v[:, W2:]], axis=0).astype(BF)

        loop(F, pack)
        us[s][f] = pb[s, f]
        nls[s][f] = nb[s]

        def send_p(i):
            q = peer(i + 1)
            rcopy(pb.at[s, q], us[s].at[f], p_s.at[s], p_r.at[s], (d, q)).start()
            rcopy(nb.at[s], nls[s].at[f], w_s.at[s], w_r.at[s], (d, q)).start()

        loop(F - 1, send_p)
        if s == 0:
            send_rest(2)
        if s == 1:
            start_third(0)
        if s + 1 < S:
            statistics(s)
        else:
            start_third(1)

    land_third(0)
    forward_third(1)
    start_third(2)
    land_third(1)
    forward_third(2)
    land_third(2)
    for h in range(2):
        for cp in halves_of_sum[h] + sum_gathers[h]:
            cp.wait_send()
    ahead.wait_send()
    for s in range(S):
        for cp in up_copies[s]:
            cp.wait_send()
        for cp in roots[s]:
            cp.wait_send()
        rests[s].wait_send()
        shares(s).wait_send()
        rcopy(pb.at[s, others(F - 1)], us[s].at[others(F - 1)], p_s.at[s], p_r.at[s], right).wait_send()
    for cp in landed + [tab_copy] + list(out_copies.values()):
        cp.wait()


def finish_kernel(nb, per, tab, *refs):
    ups, (nm, a0, a1, a2, sl, sr, left, right, up_o, left_o, right_o, acc_o) = refs[:4], refs[4:]
    step = pl.program_id(0)
    for b in range(nb):
        at = tab[4, step * nb + b]
        norms = nm[0, at] + nm[1, at] + nm[2, at] + nm[3, at]
        factor = jnp.sqrt(norms[:, 0:1] / (norms[:, 1:2] + 1e-06))
        parts = []
        for e in range(4):
            v = ups[e][at].astype(F32) * factor
            parts.append(jnp.concatenate([v[:8], v[8:]], axis=1))
        up_o[b] = jnp.concatenate(parts, axis=0).astype(BF)
    rank = jnp.full(acc_o.shape, tab[3, step // per], jnp.int32)
    acc_o[...] = jnp.where(rank == 0, a0[...], jnp.where(rank == 1, a1[...], a2[...]))
    left_o[...] = 0.95 * left[...] + 0.05 * sl[...].astype(F32)
    right_o[...] = 0.95 * right[...] + 0.05 * sr[...].astype(F32)


def body(grad_parts, left_stats, right_stats, accum, left_root, right_root, owner_slot):
    N = owner_slot.shape[0]
    F = lax.axis_size("fsdp")
    S = left_stats.shape[0]
    W = left_stats.shape[4]
    SH = F * 8
    H = N // 2
    W2 = W // 2
    hbm = pl.BlockSpec(memory_space=pl.ANY)
    vmem = pl.BlockSpec(memory_space=pltpu.VMEM)
    half = pltpu.VMEM((H, 16, W2), BF)
    whole = pltpu.VMEM((N + 1, 16, W // 4), BF)
    dma = pltpu.SemaphoreType.DMA
    share = jax.ShapeDtypeStruct((S, SH, W), BF)
    sl, sr, a0, a1, a2, up0, up1, up2, up3, nm, tab = pl.pallas_call(
        functools.partial(step_kernel, N, S, F, W),
        out_shape=(share, share) + (jax.ShapeDtypeStruct((SH, W), F32),) * 3
                  + (jax.ShapeDtypeStruct((N, 16, W2), BF),) * 4 + (
                   jax.ShapeDtypeStruct((4, N, 1, 128), F32),
                   jax.ShapeDtypeStruct((8, 128), jnp.int32)),
        in_specs=[vmem, hbm, hbm, hbm, hbm],
        out_specs=(hbm,) * 11,
        scratch_shapes=[pltpu.VMEM((N, 32, W), BF)]
        + [half] * 8
        + [whole] * 8
        + [
            pltpu.VMEM((S, F, 32, W), BF),
            pltpu.VMEM((S, F, 32, W), BF),
            pltpu.VMEM((4, S, SH, W), BF),
            pltpu.VMEM((F * 32, W), BF),
            pltpu.VMEM((S, SH, W), BF),
            pltpu.VMEM((S, SH, W), BF),
            pltpu.VMEM((S, SH, W), F32),
            pltpu.VMEM((SH, F * 32), BF),
            pltpu.VMEM((SH, W), BF),
            pltpu.VMEM((SH, W), F32),
            pltpu.VMEM((SH, F * 32), BF),
            pltpu.VMEM((SH, W), BF),
            pltpu.VMEM((SH, W), F32),
            pltpu.VMEM((SH, W), BF),
            pltpu.VMEM((SH, W), BF),
            pltpu.VMEM((S, F, 16, W2), BF),
            pltpu.VMEM((F + 1, 16, W2), BF),
            pltpu.VMEM((F + 1, 16, W2), BF),
            pltpu.VMEM((F + 1, 16, W2), BF),
            pltpu.VMEM((4, N, 16, W2), BF),
            pltpu.VMEM((S, 1, 128), F32),
            pltpu.VMEM((F + 1, 1, 128), F32),
            pltpu.VMEM((F + 1, 1, 128), F32),
            pltpu.VMEM((F + 1, 1, 128), F32),
            pltpu.VMEM((4, N, 1, 128), F32),
            pltpu.VMEM((8, 128), jnp.int32),
            pltpu.SMEM((8, 128), jnp.int32),
        ]
        + [
            dma((2, 6)), dma((2, 6)), dma((2, 4)), dma((2, 4)), dma((S, 4)), dma((S, 4)),
            dma((S + 1,)), dma((S + 1,)), dma((S,)), dma((S,)), dma((S,)), dma((S,)), dma((S, 3)), dma((S, 3)),
            dma((S, 4)), dma((S, 4)), dma((5 + S,)), dma((9, S)),
        ],
        compiler_params=pltpu.CompilerParams(
            collective_id=0, has_side_effects=True, vmem_limit_bytes=STEP_VMEM
        ),
        name="shampoo_step",
    )(
        owner_slot[None, :], grad_parts[0],
        left_root.reshape(S, SH, W), right_root.reshape(S, SH, W), accum.reshape(S, SH, W),
    )
    rows = S * SH
    K = 2 * S if N % (2 * S) == 0 and (rows // (2 * S)) % 16 == 0 else S
    nb, rb = N // K, rows // K
    per = K // S
    flat = pl.BlockSpec((rb, W), lambda i, tab: (i, 0))
    ranked = pl.BlockSpec((rb, W), lambda i, tab: (tab[3, i // per] * per + i % per, 0))
    one_rank = pl.BlockSpec((rb, W), lambda i, tab: (i % per, 0))

    def full(shape):
        return pl.BlockSpec(shape, lambda i, tab: (0,) * len(shape))

    stat = jax.ShapeDtypeStruct((rows, W), F32)
    update, left_out, right_out, accu_out = pl.pallas_call(
        functools.partial(finish_kernel, nb, per),
        grid_spec=pltpu.PrefetchScalarGridSpec(
            num_scalar_prefetch=1,
            grid=(K,),
            in_specs=[full((N, 16, W2))] * 4
            + [full((4, N, 1, 128))]
            + [one_rank] * 3
            + [ranked] * 2
            + [flat] * 2,
            out_specs=(pl.BlockSpec((nb, 32, W), lambda i, tab: (i, 0, 0)), flat, flat, flat),
        ),
        out_shape=(jax.ShapeDtypeStruct((N, 32, W), BF), stat, stat, stat),
        compiler_params=pltpu.CompilerParams(vmem_limit_bytes=FINISH_VMEM),
        name="shampoo_finish",
    )(
        tab, up0, up1, up2, up3, nm, a0, a1, a2, sl.reshape(rows, W), sr.reshape(rows, W),
        left_stats.reshape(rows, W), right_stats.reshape(rows, W),
    )
    layout = left_stats.shape
    return (update, left_out.reshape(layout), right_out.reshape(layout), accu_out.reshape(layout))


def solution(mesh):
    spread = P("fsdp", None, "dp", None, None)
    return jax.shard_map(
        body,
        mesh=mesh,
        in_specs=(P("dp", None, "fsdp", None),) + (spread,) * 5 + (P(),),
        out_specs=(P(None, "fsdp", None), spread, spread, spread),
        check_vma=False,
    )
```

```python
import functools

import jax
import jax.numpy as jnp
from jax import lax
from jax.experimental import pallas as pl
from jax.experimental.pallas import tpu as pltpu
from jax.sharding import PartitionSpec as P

MESH = pl.DeviceIdType.MESH
BF = jnp.bfloat16
F32 = jnp.float32
STEP = 5
STEP_VMEM = 45 << 20
FINISH_VMEM = 18 << 20


def dot(a, b):
    return jnp.dot(a, b, preferred_element_type=F32)


def dot_t(a, b):
    return lax.dot_general(a, b, (((1,), (1,)), ((), ())), preferred_element_type=F32)


def step_kernel(
    N, S, F, W,
    own_ref, gp_in, lr, rr, ac,
    sl_out, sr_out, an_0, an_1, an_2, up_0, up_1, up_2, up_3, nm_out, tab_out,
    gp, ra, rb, fa_raw, fb_raw, ca, cb, fa_comb, fb_comb,
    red_own_0, red_own_1, red_l_0, red_l_1, red_r_0, red_r_1, red_o_0, red_o_1,
    sb, gb, rraw, rn, rv, lv, av, sel, hf, pv, gct, gmb, anb, ls, rs_,
    pb, u_0, u_1, u_2, uall, nb, nl_0, nl_1, nl_2, nall, tab_v, tab,
    rs_s, rs_r, ag_s, ag_r, rt_s, rt_r, g_s, g_r, p_s, p_r, w_s, w_r, n_s, n_r, u_s, u_r, loc, outs,
):
    H = N // 2
    W2, W4 = W // 2, W // 4
    B = F * 32
    SH = F * 8
    T = 256 if W % 256 == 0 else W
    NT = W // T
    nx = 4 if F >= 32 else 2
    nz = F // (2 * nx)
    d = lax.axis_index("dp")
    f = lax.axis_index("fsdp")
    z = f // (2 * nx)
    x = (f // 2) % nx
    c = f % 2
    e1, e2, e3 = lax.rem(d + 1, 4), lax.rem(d + 2, 4), lax.rem(d + 3, 4)
    right, left, opp = (e1, f), (e3, f), (e2, f)
    lo, hi = pl.ds(0, H), pl.ds(H, H)

    def peer(i):
        o = lax.rem(i * STEP, F)
        pz = lax.rem(z + o // (2 * nx), nz)
        px = lax.rem(x + (o // 2) % nx, nx)
        pc = lax.rem(c + o % 2, 2)
        return (pz * nx + px) * 2 + pc

    def rcopy(src, dst, ss, rs, dev):
        return pltpu.make_async_remote_copy(
            src_ref=src, dst_ref=dst, send_sem=ss, recv_sem=rs, device_id=dev, device_id_type=MESH
        )

    def rows(e):
        return pl.ds(pl.multiple_of((e // 2) * 16, 16), 16)

    def cols(e):
        return pl.ds(pl.multiple_of((e % 2) * W2, W2), W2)

    def within(v, top):
        return jnp.minimum(jnp.maximum(v, 0), top)

    def cols4(e, h):
        return pl.ds(pl.multiple_of((e % 2) * W2 + h * W4, W4), W4)

    def part(h):
        return pl.ds(h * W4, W4)

    def loop(n, fn, unroll=4):
        unroll = n if n == F - 1 else unroll
        unroll = unroll if n % unroll == 0 else 1
        lax.fori_loop(0, n, lambda i, _: (fn(i), 0)[1], 0, unroll=unroll)

    ld_g = pltpu.make_async_copy(gp_in, gp, loc.at[4 + S])
    ld_g.start()
    ld_l = pltpu.make_async_copy(lr, lv, loc.at[0])
    ld_l.start()
    ld_a = pltpu.make_async_copy(ac, av, loc.at[1])
    ld_a.start()
    ld_r = pltpu.make_async_copy(rr, rv, loc.at[2])
    ld_r.start()

    barrier = pltpu.get_barrier_semaphore()

    def greet(i):
        pl.semaphore_signal(barrier, inc=1, device_id=(d, peer(i + 1)), device_id_type=MESH)

    for dev in (right, left, opp):
        pl.semaphore_signal(barrier, inc=1, device_id=dev, device_id_type=MESH)
    loop(F - 1, greet)
    red_own, red_l = (red_own_0, red_own_1), (red_l_0, red_l_1)
    red_r, red_o = (red_r_0, red_r_1), (red_o_0, red_o_1)
    pl.semaphore_wait(barrier, F + 2)

    def tables():
        lanes = 128

        def iota(shape, dim):
            return lax.broadcasted_iota(jnp.int32, shape, dim).astype(F32)

        def count(cond, axis):
            return jnp.sum(jnp.where(cond, 1.0, 0.0), axis=axis, keepdims=True)

        down, along = iota((N, N), 0), iota((N, N), 1)
        own_r = own_ref[...].astype(F32)
        own_rr = jnp.broadcast_to(own_r, (N, N))
        own_c = jnp.sum(jnp.where(down == along, own_rr, 0.0), axis=1, keepdims=True)
        own_cc = jnp.broadcast_to(own_c, (N, N))
        q_r = jnp.floor((own_r + 0.5) * (1.0 / S))
        q_c = jnp.floor((own_c + 0.5) * (1.0 / S))
        same = jnp.broadcast_to(q_c, (N, N)) == jnp.broadcast_to(q_r, (N, N))
        rank_r = count(same & (own_cc < own_rr), 0)
        rank_c = count(same & (own_rr < own_cc), 1)
        rk_r = jnp.broadcast_to(rank_r, (N, N))
        rk_c = jnp.broadcast_to(rank_c, (N, N))
        pos_r = count((rk_c < rk_r) | ((rk_c == rk_r) & (down < along)), 0)
        pos_c = count((rk_r < rk_c) | ((rk_r == rk_c) & (along < down)), 1)
        lane = iota((N, lanes), 1)
        block = iota((N, lanes), 0)
        lane_q = jnp.floor((lane + 0.5) * (1.0 / S))
        lane_r = lane - S * lane_q
        qw = jnp.broadcast_to(q_c, (N, lanes))
        rw = jnp.broadcast_to(rank_c, (N, lanes))
        ow = jnp.broadcast_to(own_c, (N, lanes))
        pw = jnp.broadcast_to(pos_c, (N, lanes))
        inv = jnp.min(
            jnp.where((qw == lane_q) & (rw == lane_r), block, float(N)), axis=0, keepdims=True
        )
        ord_q = jnp.sum(jnp.where(pw == lane, qw, 0.0), axis=0, keepdims=True)
        ord_r = jnp.sum(jnp.where(pw == lane, rw, 0.0), axis=0, keepdims=True)
        base = (f * S).astype(F32)
        here = qw == f.astype(F32)
        total = count(here, 0)
        low = count(here & (ow < base + lane), 0)
        used = count(ow == base + lane, 0)
        rank_s = jnp.where(used > 0.5, low, total + lane[0:1] - low)
        tab_v[0:1, :] = inv.astype(jnp.int32)
        tab_v[1:2, :] = ord_q.astype(jnp.int32)
        tab_v[2:3, :] = ord_r.astype(jnp.int32)
        tab_v[3:4, :] = rank_s.astype(jnp.int32)
        tab_v[4:5, :] = jnp.zeros((1, lanes), jnp.int32)
        tab_v[4:5, 0:N] = pos_r.astype(jnp.int32)
        tab_v[5:8, :] = jnp.zeros((3, lanes), jnp.int32)

    def sums(h):
        p, ss, rs = part(h), rs_s, rs_r
        every_a = (slice(None), slice(None), p)
        return (
            rcopy(gp_in.at[lo, rows(e2), cols4(e2, h)], ra.at[every_a], ss.at[h, 0], rs.at[h, 0], right),
            rcopy(gp_in.at[hi, rows(e2), cols4(e2, h)], rb.at[every_a], ss.at[h, 1], rs.at[h, 1], left),
            rcopy(gp_in.at[hi, rows(e1), cols4(e1, h)], fb_raw.at[every_a], ss.at[h, 2], rs.at[h, 2], right),
            rcopy(gp_in.at[lo, rows(e3), cols4(e3, h)], fa_raw.at[every_a], ss.at[h, 3], rs.at[h, 3], left),
            rcopy(ca.at[every_a], fa_comb.at[every_a], ss.at[h, 4], rs.at[h, 4], right),
            rcopy(cb.at[every_a], fb_comb.at[every_a], ss.at[h, 5], rs.at[h, 5], left),
        )

    def relay(h):
        c, p = halves_of_sum[h], part(h)
        c[0].wait_recv()

        def add_a(b):
            ca[b, :, p] = (ra[b, :, p].astype(F32) + gp[b, rows(e1), cols4(e1, h)].astype(F32)).astype(BF)

        loop(H, add_a, 3)
        c[4].start()
        c[1].wait_recv()

        def add_b(b):
            cb[b, :, p] = (
                rb[b, :, p].astype(F32) + gp[H + b, rows(e3), cols4(e3, h)].astype(F32)
            ).astype(BF)

        loop(H, add_b, 3)
        c[5].start()

    def total(h):
        c, p = halves_of_sum[h], part(h)
        c[3].wait_recv()
        c[4].wait_recv()

        def fin_a(b):
            own = gp[b, rows(d), cols4(d, h)].astype(F32)
            red_own[h][b] = (
                own + fa_raw[b, :, p].astype(F32) + fa_comb[b, :, p].astype(F32)
            ).astype(BF)

        loop(H, fin_a, 3)
        c[2].wait_recv()
        c[5].wait_recv()

        def fin_b(b):
            own = gp[H + b, rows(d), cols4(d, h)].astype(F32)
            red_own[h][H + b] = (
                own + fb_raw[b, :, p].astype(F32) + fb_comb[b, :, p].astype(F32)
            ).astype(BF)

        loop(H, fin_b, 3)

    halves_of_sum = [sums(h) for h in range(2)]
    for k in range(4):
        halves_of_sum[0][k].start()

    every = pl.ds(0, N)

    def gathers(h):
        return (
            rcopy(red_own[h].at[every], red_l[h].at[every], ag_s.at[h, 0], ag_r.at[h, 0], right),
            rcopy(red_own[h].at[every], red_r[h].at[every], ag_s.at[h, 1], ag_r.at[h, 1], left),
            rcopy(red_l[h].at[lo], red_o[h].at[lo], ag_s.at[h, 2], ag_r.at[h, 2], right),
            rcopy(red_r[h].at[hi], red_o[h].at[hi], ag_s.at[h, 3], ag_r.at[h, 3], left),
        )

    sum_gathers = [gathers(h) for h in range(2)]

    def start_gather(h):
        sum_gathers[h][0].start()
        sum_gathers[h][1].start()

    def forward_gather(h):
        sum_gathers[h][0].wait_recv()
        sum_gathers[h][2].start()
        sum_gathers[h][1].wait_recv()
        sum_gathers[h][3].start()

    HR = SH // 2
    up_, dn_ = pl.ds(0, HR), pl.ds(HR, HR)

    def root(s):
        return (
            rcopy(rraw.at[d, s], rraw.at[d, s], rt_s.at[s, 0], rt_r.at[s, 0], right),
            rcopy(rraw.at[d, s], rraw.at[d, s], rt_s.at[s, 1], rt_r.at[s, 1], left),
            rcopy(rraw.at[e3, s, up_], rraw.at[e3, s, up_], rt_s.at[s, 2], rt_r.at[s, 2], right),
            rcopy(rraw.at[e1, s, dn_], rraw.at[e1, s, dn_], rt_s.at[s, 3], rt_r.at[s, 3], left),
        )

    roots = [root(s) for s in range(S)]

    def start_root(s):
        roots[s][0].start()
        roots[s][1].start()

    def forward_root(s):
        roots[s][0].wait_recv()
        roots[s][2].start()
        roots[s][1].wait_recv()
        roots[s][3].start()

    def place(red, e, h):
        def one(q):
            for s in range(S):
                sb[s, q, rows(e), cols4(e, h)] = red[h][within(tab[0, q * S + s], N)]

        loop(F, one)

    def send_eighth(e, h):
        def one(i):
            q = peer(i + 1)
            rcopy(
                sb.at[:, q, rows(e), cols4(e, h)],
                gb.at[:, f, rows(e), cols4(e, h)],
                g_s.at[S], g_r.at[S], (d, q),
            ).start()

        loop(F - 1, one)

    def send_rest(s):
        def one(i):
            q = peer(i + 1)
            for r, c in ((rows(e3), cols4(e3, 1)), (rows(e1), cols4(e1, 1)), (rows(e2), cols(e2))):
                rcopy(sb.at[s, q, r, c], gb.at[s, f, r, c], g_s.at[s], g_r.at[s], (d, q)).start()

        loop(F - 1, one)

    def others(n):
        return pl.ds(0, n)

    ahead = rcopy(
        sb.at[:, others(F - 1), pl.ds(0, 16), :], gb.at[:, others(F - 1), pl.ds(0, 16), :],
        g_s.at[S], g_r.at[S], right,
    )
    rests = [
        rcopy(
            sb.at[s, others(F - 1), pl.ds(0, 16), :], gb.at[s, others(F - 1), pl.ds(0, 16), :],
            g_s.at[s], g_r.at[s], right,
        )
        for s in range(S)
    ]

    ld_g.wait()
    relay(0)
    for k in range(4):
        halves_of_sum[1][k].start()
    for ref in red_own + red_l + red_r + red_o:
        ref[N] = jnp.zeros((16, W4), BF)
    us = (u_0, u_1, u_2)
    for ref in us:
        ref[F] = jnp.zeros((16, W2), BF)
    nls = (nl_0, nl_1, nl_2)
    for ref in nls:
        ref[F] = jnp.zeros((1, 128), F32)
    pick = lax.broadcasted_iota(jnp.int32, (SH, B), 0)
    at = lax.broadcasted_iota(jnp.int32, (SH, B), 1)
    sel[...] = jnp.where(at == (pick // 8) * 32 + d * 8 + pick % 8, 1.0, 0.0).astype(BF)
    tables()
    to_scalars = pltpu.make_async_copy(tab_v, tab, loc.at[3])
    to_scalars.start()
    to_scalars.wait()
    perm = []
    for r in range(S):
        k = jnp.int32(0)
        for s in range(1, S):
            k = jnp.where(tab[3, s] == r, s, k)
        perm.append(within(k, S - 1))
    total(0)
    start_gather(0)
    place(red_own, d, 0)
    send_eighth(d, 0)
    relay(1)
    total(1)
    start_gather(1)
    place(red_own, d, 1)
    send_eighth(d, 1)
    ld_r.wait()

    def reorder(t):
        part = pl.ds(pl.multiple_of(t * 16, 16), 16)
        for r in range(S):
            rraw[d, r, part, :] = rv[perm[r], part, :]

    loop(SH // 16, reorder)
    forward_gather(0)
    place(red_l, e3, 0)
    send_eighth(e3, 0)
    place(red_r, e1, 0)
    send_eighth(e1, 0)
    forward_gather(1)
    start_root(0)
    start_root(1)
    place(red_l, e3, 1)
    place(red_r, e1, 1)
    for h in range(2):
        sum_gathers[h][2].wait_recv()
        sum_gathers[h][3].wait_recv()
        place(red_o, e2, h)
    selfs = [pltpu.make_async_copy(sb.at[s, f], gb.at[s, f], loc.at[4 + s]) for s in range(S)]
    send_rest(0)
    for s in range(S):
        selfs[s].start()
    send_rest(1)
    forward_root(0)
    start_root(2)
    ld_l.wait()
    ld_a.wait()

    def tile(j):
        return pl.ds(pl.multiple_of(j * T, T), T)

    def gcols(s, j):
        return gb[s, :, :, tile(j)].reshape(B, T)

    def grows(s, j):
        return gb[s, pl.ds(j * (T // 32), T // 32)].reshape(T, W)

    out_copies = {}

    def put(src, dst, k, s):
        cp = pltpu.make_async_copy(src, dst, outs.at[k, s])
        cp.start()
        out_copies[id(src)] = cp

    def free(src):
        cp = out_copies.pop(id(src), None)
        if cp is not None:
            cp.wait()

    def third(t):
        n = N // S
        own = pl.ds(t * n, n)
        a, b = pl.ds(t * n, n // 2), pl.ds(t * n + n // 2, n - n // 2)
        return (
            rcopy(uall.at[d, own], uall.at[d, own], u_s.at[t, 0], u_r.at[t, 0], right),
            rcopy(uall.at[d, own], uall.at[d, own], u_s.at[t, 1], u_r.at[t, 1], left),
            rcopy(uall.at[e3, a], uall.at[e3, a], u_s.at[t, 2], u_r.at[t, 2], right),
            rcopy(uall.at[e1, b], uall.at[e1, b], u_s.at[t, 3], u_r.at[t, 3], left),
        ) + tuple(
            rcopy(nall.at[d, own], nall.at[d, own], n_s.at[t, k], n_r.at[t, k], dev)
            for k, dev in enumerate((right, left, opp))
        )

    up_copies = [third(t) for t in range(S)]

    def shares(t):
        return rcopy(
            nls[t].at[others(F - 1)], nls[t].at[others(F - 1)], w_s.at[t], w_r.at[t], right
        )

    def start_third(t):
        rcopy(
            pb.at[t, others(F - 1)], us[t].at[others(F - 1)], p_s.at[t], p_r.at[t], right
        ).wait_recv()
        shares(t).wait_recv()

        def choose(i):
            j = t * (N // S) + i
            q, r = within(tab[1, j], F), tab[2, j]
            v = us[0][jnp.where(r == 0, q, F)].astype(F32)
            n = nls[0][jnp.where(r == 0, q, F)]
            for k in range(1, t + 1):
                v = v + us[k][jnp.where(r == k, q, F)].astype(F32)
                n = n + nls[k][jnp.where(r == k, q, F)]
            uall[d, j] = v.astype(BF)
            nall[d, j] = n

        loop(N // S, choose)
        for k in (0, 1, 4, 5, 6):
            up_copies[t][k].start()

    def forward_third(t):
        up_copies[t][0].wait_recv()
        up_copies[t][2].start()
        up_copies[t][1].wait_recv()
        up_copies[t][3].start()

    def statistics(s):
        free(ls)
        free(rs_)

        def left_stat(j):
            g = grows(s, j)
            ls[:, tile(j)] = dot_t(gmb[...], g).astype(BF)
            gct[:, tile(j)] = dot_t(sel[...], g).astype(BF)

        loop(NT, left_stat, 4)
        put(ls, sl_out.at[s], 1, s)

        def right_stat(j):
            rs_[:, tile(j)] = dot(gct[...], gcols(s, j)).astype(BF)

        loop(NT, right_stat, 4)
        put(rs_, sr_out.at[s], 2, s)

    def land_third(t):
        for k in (2, 3, 4, 5, 6):
            up_copies[t][k].wait_recv()
        own = pl.ds(t * (N // S), N // S)
        pairs = [(uall.at[e, own], up.at[own]) for e, up in enumerate((up_0, up_1, up_2, up_3))]
        for k, (src, dst) in enumerate(pairs + [(nall.at[:, own], nm_out.at[:, own])]):
            cp = pltpu.make_async_copy(src, dst, outs.at[4 + k, t])
            cp.start()
            landed.append(cp)

    landed = []
    tab_copy = pltpu.make_async_copy(tab_v, tab_out, outs.at[3, 0])
    tab_copy.start()
    ahead.wait_recv()
    for s in range(S):
        rests[s].wait_recv()
        selfs[s].wait()

        def halves(j):
            hf[:, tile(j)] = dot(lv[perm[s]], gcols(s, j)).astype(BF)

        loop(NT, halves, 4)

        def mine(j, dn):
            g = dot(sel[...], gcols(s, j))
            gmb[:, tile(j)] = g.astype(BF)
            an = av[perm[s], :, tile(j)] + g * g
            anb[:, tile(j)] = an
            dr = g * lax.rsqrt(an)
            return dn + jnp.sum(dr * dr)

        free(anb)
        dn = lax.fori_loop(0, NT, mine, jnp.float32(0), unroll=NT)
        put(anb, (an_0, an_1, an_2)[s], 0, s)

        if s + 1 < S:
            forward_root(s + 1)
        else:
            forward_third(0)
            statistics(s)
        roots[s][2].wait_recv()
        roots[s][3].wait_recv()

        def weave(t):
            part16 = pl.ds(pl.multiple_of(t * 16, 16), 16)
            quarter = [rraw[e, s, part16, :].astype(F32) for e in range(4)]
            for h in range(2):
                rows32 = jnp.concatenate([p[8 * h : 8 * h + 8] for p in quarter], axis=0)
                rn[pl.ds(pl.multiple_of(t * 64 + 32 * h, 32), 32), :] = rows32.astype(BF)

        loop(F // 2, weave)

        def prec(j, pn):
            p = dot(hf[...], rn[:, tile(j)])
            pv[:, tile(j)] = p
            return pn + jnp.sum(p * p)

        pn = lax.fori_loop(0, NT, prec, jnp.float32(0), unroll=NT)

        lane = lax.broadcasted_iota(jnp.int32, (1, 128), 1)
        nb[s] = jnp.where(lane == 0, dn, jnp.where(lane == 1, pn, 0.0))

        def pack(q):
            v = pv[pl.ds(pl.multiple_of(q * 8, 8), 8), :]
            pb[s, q] = jnp.concatenate([v[:, :W2], v[:, W2:]], axis=0).astype(BF)

        loop(F, pack)
        us[s][f] = pb[s, f]
        nls[s][f] = nb[s]

        def send_p(i):
            q = peer(i + 1)
            rcopy(pb.at[s, q], us[s].at[f], p_s.at[s], p_r.at[s], (d, q)).start()
            rcopy(nb.at[s], nls[s].at[f], w_s.at[s], w_r.at[s], (d, q)).start()

        loop(F - 1, send_p)
        if s == 0:
            send_rest(2)
        if s == 1:
            start_third(0)
        if s + 1 < S:
            statistics(s)
        else:
            start_third(1)

    land_third(0)
    forward_third(1)
    start_third(2)
    land_third(1)
    forward_third(2)
    land_third(2)
    for h in range(2):
        for cp in halves_of_sum[h] + sum_gathers[h]:
            cp.wait_send()
    ahead.wait_send()
    for s in range(S):
        for cp in up_copies[s]:
            cp.wait_send()
        for cp in roots[s]:
            cp.wait_send()
        rests[s].wait_send()
        shares(s).wait_send()
        rcopy(pb.at[s, others(F - 1)], us[s].at[others(F - 1)], p_s.at[s], p_r.at[s], right).wait_send()
    for cp in landed + [tab_copy] + list(out_copies.values()):
        cp.wait()


def finish_kernel(nb, per, tab, *refs):
    ups, (nm, a0, a1, a2, sl, sr, left, right, up_o, left_o, right_o, acc_o) = refs[:4], refs[4:]
    step = pl.program_id(0)
    for b in range(nb):
        at = tab[4, step * nb + b]
        norms = nm[0, at] + nm[1, at] + nm[2, at] + nm[3, at]
        factor = jnp.sqrt(norms[:, 0:1] / (norms[:, 1:2] + 1e-06))
        parts = []
        for e in range(4):
            v = ups[e][at].astype(F32) * factor
            parts.append(jnp.concatenate([v[:8], v[8:]], axis=1))
        up_o[b] = jnp.concatenate(parts, axis=0).astype(BF)
    rank = jnp.full(acc_o.shape, tab[3, step // per], jnp.int32)
    acc_o[...] = jnp.where(rank == 0, a0[...], jnp.where(rank == 1, a1[...], a2[...]))
    left_o[...] = 0.95 * left[...] + 0.05 * sl[...].astype(F32)
    right_o[...] = 0.95 * right[...] + 0.05 * sr[...].astype(F32)


def body(grad_parts, left_stats, right_stats, accum, left_root, right_root, owner_slot):
    N = owner_slot.shape[0]
    F = lax.axis_size("fsdp")
    S = left_stats.shape[0]
    W = left_stats.shape[4]
    SH = F * 8
    H = N // 2
    W2 = W // 2
    hbm = pl.BlockSpec(memory_space=pl.ANY)
    vmem = pl.BlockSpec(memory_space=pltpu.VMEM)
    half = pltpu.VMEM((H, 16, W2), BF)
    whole = pltpu.VMEM((N + 1, 16, W // 4), BF)
    dma = pltpu.SemaphoreType.DMA
    share = jax.ShapeDtypeStruct((S, SH, W), BF)
    sl, sr, a0, a1, a2, up0, up1, up2, up3, nm, tab = pl.pallas_call(
        functools.partial(step_kernel, N, S, F, W),
        out_shape=(share, share) + (jax.ShapeDtypeStruct((SH, W), F32),) * 3
                  + (jax.ShapeDtypeStruct((N, 16, W2), BF),) * 4 + (
                   jax.ShapeDtypeStruct((4, N, 1, 128), F32),
                   jax.ShapeDtypeStruct((8, 128), jnp.int32)),
        in_specs=[vmem, hbm, hbm, hbm, hbm],
        out_specs=(hbm,) * 11,
        scratch_shapes=[pltpu.VMEM((N, 32, W), BF)]
        + [half] * 8
        + [whole] * 8
        + [
            pltpu.VMEM((S, F, 32, W), BF),
            pltpu.VMEM((S, F, 32, W), BF),
            pltpu.VMEM((4, S, SH, W), BF),
            pltpu.VMEM((F * 32, W), BF),
            pltpu.VMEM((S, SH, W), BF),
            pltpu.VMEM((S, SH, W), BF),
            pltpu.VMEM((S, SH, W), F32),
            pltpu.VMEM((SH, F * 32), BF),
            pltpu.VMEM((SH, W), BF),
            pltpu.VMEM((SH, W), F32),
            pltpu.VMEM((SH, F * 32), BF),
            pltpu.VMEM((SH, W), BF),
            pltpu.VMEM((SH, W), F32),
            pltpu.VMEM((SH, W), BF),
            pltpu.VMEM((SH, W), BF),
            pltpu.VMEM((S, F, 16, W2), BF),
            pltpu.VMEM((F + 1, 16, W2), BF),
            pltpu.VMEM((F + 1, 16, W2), BF),
            pltpu.VMEM((F + 1, 16, W2), BF),
            pltpu.VMEM((4, N, 16, W2), BF),
            pltpu.VMEM((S, 1, 128), F32),
            pltpu.VMEM((F + 1, 1, 128), F32),
            pltpu.VMEM((F + 1, 1, 128), F32),
            pltpu.VMEM((F + 1, 1, 128), F32),
            pltpu.VMEM((4, N, 1, 128), F32),
            pltpu.VMEM((8, 128), jnp.int32),
            pltpu.SMEM((8, 128), jnp.int32),
        ]
        + [
            dma((2, 6)), dma((2, 6)), dma((2, 4)), dma((2, 4)), dma((S, 4)), dma((S, 4)),
            dma((S + 1,)), dma((S + 1,)), dma((S,)), dma((S,)), dma((S,)), dma((S,)), dma((S, 3)), dma((S, 3)),
            dma((S, 4)), dma((S, 4)), dma((5 + S,)), dma((9, S)),
        ],
        compiler_params=pltpu.CompilerParams(
            collective_id=0, has_side_effects=True, vmem_limit_bytes=STEP_VMEM
        ),
        name="shampoo_step",
    )(
        owner_slot[None, :], grad_parts[0],
        left_root.reshape(S, SH, W), right_root.reshape(S, SH, W), accum.reshape(S, SH, W),
    )
    rows = S * SH
    K = 2 * S if N % (2 * S) == 0 and (rows // (2 * S)) % 16 == 0 else S
    nb, rb = N // K, rows // K
    per = K // S
    flat = pl.BlockSpec((rb, W), lambda i, tab: (i, 0))
    ranked = pl.BlockSpec((rb, W), lambda i, tab: (tab[3, i // per] * per + i % per, 0))
    one_rank = pl.BlockSpec((rb, W), lambda i, tab: (i % per, 0))

    def full(shape):
        return pl.BlockSpec(shape, lambda i, tab: (0,) * len(shape))

    stat = jax.ShapeDtypeStruct((rows, W), F32)
    update, left_out, right_out, accu_out = pl.pallas_call(
        functools.partial(finish_kernel, nb, per),
        grid_spec=pltpu.PrefetchScalarGridSpec(
            num_scalar_prefetch=1,
            grid=(K,),
            in_specs=[full((N, 16, W2))] * 4
            + [full((4, N, 1, 128))]
            + [one_rank] * 3
            + [ranked] * 2
            + [flat] * 2,
            out_specs=(pl.BlockSpec((nb, 32, W), lambda i, tab: (i, 0, 0)), flat, flat, flat),
        ),
        out_shape=(jax.ShapeDtypeStruct((N, 32, W), BF), stat, stat, stat),
        compiler_params=pltpu.CompilerParams(vmem_limit_bytes=FINISH_VMEM),
        name="shampoo_finish",
    )(
        tab, up0, up1, up2, up3, nm, a0, a1, a2, sl.reshape(rows, W), sr.reshape(rows, W),
        left_stats.reshape(rows, W), right_stats.reshape(rows, W),
    )
    layout = left_stats.shape
    return (update, left_out.reshape(layout), right_out.reshape(layout), accu_out.reshape(layout))


def solution(mesh):
    spread = P("fsdp", None, "dp", None, None)
    return jax.shard_map(
        body,
        mesh=mesh,
        in_specs=(P("dp", None, "fsdp", None),) + (spread,) * 5 + (P(),),
        out_specs=(P(None, "fsdp", None), spread, spread, spread),
        check_vma=False,
    )
```
